32 devices in a mesh: fsdp: 2 (over x), ctx: 4 (over z), tp: 4 (over y, core).
Axes of the slice: x: 2, y: 2, z: 4, core: 2. Of those that a mesh axis runs over, the one named last changes fastest.
Arguments:
- inputs: bfloat16 [4, 2048, 1024], P('fsdp', 'ctx'), may hold values from -6 to 6
- cotangent: bfloat16 [4, 2048, 1024], P('fsdp', 'ctx'), may hold values from -6 to 6
- lengths: int32 [4], P('fsdp'), may hold values from 256 to 2048, as said below
- attention_gain: bfloat16 [1024], P('fsdp'), may hold values from 0.099609375 to 1.8984375
- triple_weight: bfloat16 [1024, 3, 1024], P('fsdp', None, 'tp'), may hold values from -0.1875 to 0.1875
- mixing_weight: bfloat16 [1024, 1024], P('tp', 'fsdp'), may hold values from -6 to 6
- feedforward_gain: bfloat16 [1024], P('fsdp'), may hold values from 0.099609375 to 1.8984375
- lifting_weight: bfloat16 [1024, 2, 2624], P('fsdp', None, 'tp'), may hold values from -0.1875 to 0.1875
- down_weight: bfloat16 [2624, 1024], P('tp', 'fsdp'), may hold values from -0.125 to 0.125
Outputs:
- output: bfloat16 [4, 2048, 1024], P('fsdp', 'ctx')
- input_gradient: bfloat16 [4, 2048, 1024], P('fsdp', 'ctx')
- attention_gain_gradient: float32 [1024], P('fsdp')
- triple_gradient: float32 [1024, 3, 1024], P('fsdp', None, 'tp')
- mixing_gradient: float32 [1024, 1024], P('tp', 'fsdp')
- feedforward_gain_gradient: float32 [1024], P('fsdp')
- lifting_gradient: float32 [1024, 2, 2624], P('fsdp', None, 'tp')
- down_gradient: float32 [2624, 1024], P('tp', 'fsdp')
The draws below stay inside these ranges and needn't reach their ends.
Inputs may be any that keep to these rules, and one draw needn't show every extreme that they name: `lengths`: in each aligned group of 2 sequences, one drawn at random has length 2048.
All inputs are finite; a program needn't handle non-finite values.
Results may differ from the reference program's by a relative error of at most 0.022.
Values may be sent and summed in bfloat16 or wider, within the bound.
No kernel may reach another device: no remote copies, remote signals or barrier semaphores. Data moves between devices by JAX's collectives and lax.ppermute only.
A program may use at most 192 MiB of HBM per device.

```python
import math
import jax
import jax.numpy as jnp
from jax import lax

D = 1024
H = 16
FF = 2624
LENGTH = 2048
SEQ_DEV = 2
SEQS = 4


def draw_lengths(key, part):
    key = jax.random.fold_in(key, 7)
    first_key, second_key = jax.random.split(key)
    drawn = jax.random.randint(first_key, (SEQS,), LENGTH // 8, LENGTH + 1, dtype=jnp.int32)
    chosen = jax.random.randint(second_key, (SEQS // SEQ_DEV,), 0, SEQ_DEV, dtype=jnp.int32)
    slots = jnp.arange(SEQS, dtype=jnp.int32)
    longest = slots % SEQ_DEV == jnp.repeat(chosen, SEQ_DEV, total_repeat_length=SEQS)
    return jnp.where(longest, LENGTH, drawn).astype(jnp.int32)


def level_of(own_key, extent, cuts, least, largest):
    gain = 1.0
    for position, parts in cuts:
        steps = jax.random.uniform(jax.random.fold_in(jax.random.fold_in(own_key, 6), position), (parts,), jnp.float32, least / len(cuts), largest / len(cuts))
        gain = gain * jnp.repeat(jnp.exp(steps), extent[position] // parts).reshape((-1,) + (1,) * (len(extent) - 1 - position))
    return gain


def normal_values(key, dims, deviation, limit, shards=(), kind=jnp.bfloat16):
    array = jax.random.normal(key, dims, jnp.float32) * deviation
    if len(shards) > 0:
        array = level_of(key, dims, shards, -0.22, 0.18) * array
    return jnp.clip(array, min=-limit, max=limit).astype(kind)


def setup_inputs(seed: int = 0) -> dict:
    streams_of = jax.random.split(jax.random.key(seed), 10)
    return {
        "inputs": normal_values(streams_of[0], (SEQS, LENGTH, D), 1.0, 6.0, ((0, 2), (1, 4))),
        "cotangent": normal_values(streams_of[1], (SEQS, LENGTH, D), 1.0, 6.0, ((0, 2), (1, 4))),
        "lengths": draw_lengths(jax.random.fold_in(streams_of[9], 71), 0),
        "attention_gain": jnp.clip(1.0 + 0.18 * jax.random.normal(streams_of[3], (D,), jnp.float32), 0.099609375, 1.8984375).astype(jnp.bfloat16),
        "triple_weight": normal_values(streams_of[4], (D, 3, D), D ** -0.5, 0.1875, ((0, 2), (2, 4))),
        "mixing_weight": normal_values(streams_of[5], (D, D), (max(1, 2 * D // LENGTH)) ** -0.5, 6.0, ((0, 4), (1, 2))),
        "feedforward_gain": jnp.clip(1.0 + 0.18 * jax.random.normal(streams_of[6], (D,), jnp.float32), 0.099609375, 1.8984375).astype(jnp.bfloat16),
        "lifting_weight": normal_values(streams_of[7], (D, 2, FF), D ** -0.5, 0.1875, ((0, 2), (2, 4))),
        "down_weight": normal_values(streams_of[8], (FF, D), FF ** -0.5, 0.125, ((0, 4), (1, 2))),
    }


HIGHEST = lax.Precision.HIGHEST
NORM_EPS = 1e-05
ROPE_BASE = 160000.0
MASKED = -1e+30

@jax.custom_vjp
def low(v):
    return lax.optimization_barrier(v.astype(jnp.bfloat16)).astype(jnp.float32)

@jax.custom_vjp
def low_back(v):
    return v

def low_keep(v):
    return (low(v), None)

def low_pass(kept, grad):
    return (grad,)

def back_keep(v):
    return (v, None)

def back_low(kept, grad):
    return (low(grad),)
low.defvjp(low_keep, low_pass)
low_back.defvjp(back_keep, back_low)

def layer_norm(values_in, gain_vector):
    center = values_in - lax.optimization_barrier(jnp.mean(values_in, axis=-1, keepdims=True))
    spread = lax.optimization_barrier(jnp.mean(center * center, axis=-1, keepdims=True))
    return center * lax.rsqrt(spread + NORM_EPS) * gain_vector

def rope_tables(positions, head_size):
    frequency = ROPE_BASE ** (-2.0 * jnp.arange(head_size // 2, dtype=jnp.float32) / head_size)
    angles = positions[:, None] * frequency[None, :]
    return (jnp.cos(angles), jnp.sin(angles))

def rotate(vectors, cosine, sine_table):
    half_size = vectors.shape[-1] // 2
    first_half = vectors[..., :half_size]
    second_half = vectors[..., half_size:]
    cosine = cosine[:, None, :]
    sine_table = sine_table[:, None, :]
    return jnp.concatenate([first_half * cosine - second_half * sine_table, second_half * cosine + first_half * sine_table], axis=-1)

def attention(queries, keys_all, values_all, valid_keys):
    group_size, length_all, head_count, head_size = queries.shape
    block_rows = min(512, length_all)
    block_count = length_all // block_rows
    score_scale = head_size ** (-0.5)

    def one_block(query_block):
        raw_scores = low_back(jnp.einsum('gqhd,gkhd->ghqk', query_block, keys_all, precision=HIGHEST))
        scores = jnp.where(valid_keys[:, None, None, :], raw_scores * score_scale, MASKED)
        row_peak = lax.optimization_barrier(jnp.max(scores, axis=-1, keepdims=True))
        exponent = jnp.exp(scores - row_peak)
        softmax_weights = exponent / lax.optimization_barrier(jnp.sum(exponent, axis=-1, keepdims=True))
        return jnp.einsum('ghqk,gkhd->gqhd', low(softmax_weights), values_all, precision=HIGHEST)
    blocks = queries.reshape(group_size, block_count, block_rows, head_count, head_size).transpose(1, 0, 2, 3, 4)
    mixture = lax.map(jax.checkpoint(one_block), blocks)
    return mixture.transpose(1, 0, 2, 3, 4).reshape(group_size, length_all, head_count, head_size)

def forward(inputs_float, weights, valid_keys, cosine, sine_table):
    attention_gain, triple_weight, mixing_weight, feedforward_gain, lifting_weight, down_weight = weights
    group_size, length_all, model_width = inputs_float.shape
    head_size = model_width // H
    normed = low(layer_norm(inputs_float, attention_gain))
    projected = low_back(jnp.einsum('gld,dce->glce', normed, triple_weight, precision=HIGHEST))
    head_parts = projected.reshape(group_size, length_all, 3, H, head_size)
    queries = low(rotate(head_parts[:, :, 0], cosine, sine_table))
    keys_all = low(rotate(head_parts[:, :, 1], cosine, sine_table))
    values_all = low(head_parts[:, :, 2])
    mixture = attention(queries, keys_all, values_all, valid_keys)
    mixture = low(low_back(mixture)).reshape(group_size, length_all, model_width)
    middle = inputs_float + low_back(jnp.einsum('gle,ed->gld', mixture, mixing_weight, precision=HIGHEST))
    normed_second = low(layer_norm(middle, feedforward_gain))
    lifted = low_back(jnp.einsum('gld,dcf->glcf', normed_second, lifting_weight, precision=HIGHEST))
    hidden = low(jax.nn.gelu(lifted[:, :, 0], approximate=False) * lifted[:, :, 1])
    return middle + low_back(jnp.einsum('glf,fd->gld', hidden, down_weight, precision=HIGHEST))

def reference(inputs, cotangent, lengths, attention_gain, triple_weight, mixing_weight, feedforward_gain, lifting_weight, down_weight):
    weights = tuple((weight.astype(jnp.float32) for weight in (attention_gain, triple_weight, mixing_weight, feedforward_gain, lifting_weight, down_weight)))
    positions = jnp.arange(LENGTH, dtype=jnp.int32).astype(jnp.float32)
    cosine, sine_table = rope_tables(positions, D // H)
    group_size = math.gcd(SEQS, max(1, 4096 // LENGTH))
    steps_count = SEQS // group_size
    batched = (inputs.reshape(steps_count, group_size, LENGTH, D), cotangent.reshape(steps_count, group_size, LENGTH, D), lengths.reshape(steps_count, group_size))

    def scan_step(totals, batch_part):
        inputs_part, cotangent_part, lengths_part = batch_part
        valid_keys = jnp.arange(LENGTH, dtype=jnp.int32)[None, :] < lengths_part[:, None]

        def run_layer(inputs_float, *weight_list):
            return forward(inputs_float, weight_list, valid_keys, cosine, sine_table)
        result, pullback = jax.vjp(run_layer, inputs_part.astype(jnp.float32), *weights)
        gradients = pullback(cotangent_part.astype(jnp.float32))
        running = tuple((total_sum + gradient for total_sum, gradient in zip(totals, gradients[1:])))
        return (running, (result.astype(jnp.bfloat16), gradients[0].astype(jnp.bfloat16)))
    zeros_start = tuple((jnp.zeros_like(weight) for weight in weights))
    totals, (outputs, input_gradients) = lax.scan(scan_step, zeros_start, batched)
    return (outputs.reshape(SEQS, LENGTH, D), input_gradients.reshape(SEQS, LENGTH, D), totals[0], totals[1], totals[2], totals[3], totals[4], totals[5])
```

```python
import functools

import jax
import jax.numpy as jnp
from jax import lax
from jax.experimental import pallas as pl
from jax.experimental.pallas import tpu as pltpu
from jax.sharding import PartitionSpec as P

H = 16
NORM_EPS = 1e-05
ROPE_BASE = 160000.0
MASKED = -1e30
BF = jnp.bfloat16
F32 = jnp.float32
CORE, ROW = 1, 2


def nn(a, b):
    return lax.dot_general(a, b, (((1,), (0,)), ((), ())), preferred_element_type=F32)


def nt(a, b):
    return lax.dot_general(a, b, (((1,), (1,)), ((), ())), preferred_element_type=F32)


def in_vmem():
    return pl.BlockSpec(memory_space=pltpu.VMEM)


def in_smem():
    return pl.BlockSpec(memory_space=pltpu.SMEM)


def kernel(body, scalars, arrays, outs, scratch=(), flops=0, name=None, mib=48):
    moved = sum(a.size * a.dtype.itemsize for a in arrays)
    moved += sum(jnp.dtype(t).itemsize * functools.reduce(lambda u, v: u * v, s) for s, t in outs)
    return pl.pallas_call(
        body,
        out_shape=[jax.ShapeDtypeStruct(s, t) for s, t in outs],
        in_specs=[in_smem()] * len(scalars) + [in_vmem()] * len(arrays),
        out_specs=[in_vmem()] * len(outs),
        scratch_shapes=list(scratch),
        compiler_params=pltpu.CompilerParams(vmem_limit_bytes=mib << 20),
        cost_estimate=pl.CostEstimate(flops=flops, bytes_accessed=moved, transcendentals=0),
        name=name,
    )(*scalars, *arrays)


def swap(array, axis, size, step):
    return lax.ppermute(array, axis, [(i, i ^ step) for i in range(size)])


def half_at(ref, which, half):
    return ref[:, pl.ds(pl.multiple_of(which * half, half), half)]


def norm_body(place, x, gain_own, gain_other, out):
    half = gain_own.shape[1]
    xi = place[2]
    rows = x.shape[0]
    step = 256

    def block(i, carry):
        at = pl.ds(pl.multiple_of(i * step, step), step)
        v = x[at, :].astype(F32)
        center = v - jnp.mean(v, axis=-1, keepdims=True)
        spread = jnp.mean(center * center, axis=-1, keepdims=True)
        gains = [gain_own[...].astype(F32), gain_other[...].astype(F32)]
        low = jnp.where(xi == 0, gains[0], gains[1])
        high = jnp.where(xi == 0, gains[1], gains[0])
        gain = jnp.concatenate([low, high], axis=1)
        out[at, :] = (center * lax.rsqrt(spread + NORM_EPS) * gain).astype(BF)
        return carry

    lax.fori_loop(0, rows // step, block, 0)


def project_body(rotated, place, *refs):
    if rotated:
        normed, w_own, w_other, cosine, sine, *rest = refs
    else:
        normed, w_own, w_other, *rest = refs
    outs, heads = rest[:-1], rest[-1]
    count = len(outs)
    size = outs[0].shape[0]
    half = w_own.shape[1]
    z, xi = place[0], place[2]
    tokens = normed.shape[0]
    span = 512
    for s in range(tokens // span):
        rows = slice(s * span, (s + 1) * span)
        n_own = normed[rows, pl.ds(pl.multiple_of(xi * half, half), half)]
        n_other = normed[rows, pl.ds(pl.multiple_of((1 - xi) * half, half), half)]
        acc = nt(w_own[...], n_own) + nt(w_other[...], n_other)
        for h in range(count):
            u = acc[h * size : (h + 1) * size]
            if rotated:
                u1, u2 = u[: size // 2], u[size // 2 :]
                co, si = cosine[...], sine[...]
                u = jnp.concatenate([u1 * co - u2 * si, u2 * co + u1 * si], axis=0)
            heads[h, :, rows] = u.astype(BF)
    for m in range(count):
        outs[m][...] = heads[z ^ m]


def attend_body(s, span, place, lengths, *refs):
    q, k, v = refs[0:4], refs[4:8], refs[8:12]
    o, o_full, lse = refs[12:16], refs[16], refs[17]
    keys, values, top, total = refs[18:22]
    z = place[0]
    size = q[0].shape[0]
    cols = slice(s * span, (s + 1) * span)
    for m in range(4):
        keys[z ^ m] = k[m][:, cols].T
        values[z ^ m] = v[m][:, cols]
    top[...] = jnp.full_like(top, MASKED)
    total[...] = jnp.zeros_like(total)
    o_full[...] = jnp.zeros_like(o_full)
    length = lengths[s]
    full = length // span
    rest = length - full * span

    def step(j, limit):
        key, value = keys[j], values[j]
        for m in range(4):
            st = nn(key, q[m][:, cols]) * (size**-0.5)
            if limit is not None:
                st = jnp.where(lax.broadcasted_iota(jnp.int32, st.shape, 0) < limit, st, MASKED)
            before = top[m : m + 1, :]
            peak = jnp.maximum(before, jnp.max(st, axis=0, keepdims=True))
            p = jnp.exp(st - peak)
            scale = jnp.exp(before - peak)
            top[m : m + 1, :] = peak
            total[m : m + 1, :] = total[m : m + 1, :] * scale + jnp.sum(p, axis=0, keepdims=True)
            o_full[m] = o_full[m] * scale + nn(value, p.astype(BF))

    def whole(j, carry):
        step(j, None)
        return carry

    lax.fori_loop(0, full, whole, 0)

    @pl.when(rest > 0)
    def _():
        step(full, rest)

    for m in range(4):
        result = o_full[m] / total[m : m + 1, :]
        o_full[m] = result
        o[m][...] = result.astype(BF)
        lse[m : m + 1, :] = top[m : m + 1, :] + jnp.log(total[m : m + 1, :])


def attend_back_body(s, span, place, lengths, *refs):
    q, k, v, do = refs[0:4], refs[4:8], refs[8:12], refs[12:16]
    o_full, lse, cosine, sine = refs[16:20]
    out = refs[20:24]
    keys, keys_t, values, d_query, d_key, d_value, queries, grads, delta = refs[24:]
    z = place[0]
    size = q[0].shape[0]
    cols = slice(s * span, (s + 1) * span)
    for m in range(4):
        keys[z ^ m] = k[m][:, cols].T
        keys_t[z ^ m] = k[m][:, cols]
        values[z ^ m] = v[m][:, cols].T
        queries[m] = q[m][:, cols].T
        grads[m] = do[m][...].T
        delta[m : m + 1, :] = jnp.sum(do[m][...].astype(F32) * o_full[m], axis=0, keepdims=True)
    d_query[...] = jnp.zeros_like(d_query)
    d_key[...] = jnp.zeros_like(d_key)
    d_value[...] = jnp.zeros_like(d_value)
    length = lengths[s]
    full = length // span
    rest = length - full * span
    factor = size**-0.5

    def step(j, limit):
        key, key_t, value = keys[j], keys_t[j], values[j]
        for m in range(4):
            st = nn(key, q[m][:, cols]) * factor
            if limit is not None:
                st = jnp.where(lax.broadcasted_iota(jnp.int32, st.shape, 0) < limit, st, MASKED)
            p = jnp.exp(st - lse[m : m + 1, :])
            dp = nn(value, do[m][...])
            ds = (p * (dp - delta[m : m + 1, :]) * factor).astype(BF)
            d_value[j] += nn(p.astype(BF), grads[m])
            d_key[j] += nn(ds, queries[m])
            d_query[m] += nn(key_t, ds)

    def whole(j, carry):
        step(j, None)
        return carry

    lax.fori_loop(0, full, whole, 0)

    @pl.when(rest > 0)
    def _():
        step(full, rest)

    def back(w, j):
        at = pl.ds(pl.multiple_of(j * span, span), span)
        co, si = cosine[:, at], sine[:, at]
        w1, w2 = w[: size // 2], w[size // 2 :]
        return jnp.concatenate([w1 * co + w2 * si, w2 * co - w1 * si], axis=0).astype(BF)

    for m in range(4):
        j = z ^ m
        out[m][0:size, :] = back(d_query[m], j)
        out[m][size : 2 * size, :] = back(d_key[j].T, j)
        out[m][2 * size :, :] = d_value[j].T.astype(BF)


def mix_body(place, o0, o1, o2, o3, w_own, w_other, keep, send, mixed):
    z, c, xi = place[0], place[1], place[2]
    size = o0.shape[0]
    half = w_own.shape[1]
    rows = keep.shape[0]
    for m, o in enumerate((o0, o1, o2, o3)):
        mixed[pl.ds(pl.multiple_of((z ^ m) * size, size), size), :] = o[...]
    for target, at in ((keep, c), (send, 1 - c)):
        mix = mixed[:, pl.ds(pl.multiple_of(at * rows, rows), rows)].T
        for w, hi in ((w_own, xi), (w_other, 1 - xi)):
            cols = pl.ds(pl.multiple_of(hi * half, half), half)
            target[:, cols] = nn(mix, w[...]).astype(target.dtype)


def whole_gain(gain, xi):
    own, other = gain[0:1, :].astype(F32), gain[1:2, :].astype(F32)
    low = jnp.where(xi == 0, own, other)
    high = jnp.where(xi == 0, other, own)
    return jnp.concatenate([low, high], axis=1)


def second_norm_body(place, mine, theirs, x, gain, middle, normed):
    v = x[...].astype(F32) + (mine[...].astype(F32) + theirs[...].astype(F32))
    middle[...] = v
    center = v - jnp.mean(v, axis=-1, keepdims=True)
    spread = jnp.mean(center * center, axis=-1, keepdims=True)
    normed[...] = (center * lax.rsqrt(spread + NORM_EPS) * whole_gain(gain, place[2])).astype(BF)


def feed_body(place, n_own, n_other, cot, lift_own, lift_other, down_own, down_other, *outs):
    keep, send, keep_grad, send_grad, hidden, inner, gate = outs
    c, xi = place[1], place[2]
    half = down_own.shape[1]
    rows = n_own.shape[0]
    own_cols = pl.ds(pl.multiple_of(xi * half, half), half)
    other_cols = pl.ds(pl.multiple_of((1 - xi) * half, half), half)
    parts = ((n_own, c, keep, keep_grad, 0), (n_other, 1 - c, send, send_grad, 1))
    for n, at, target, target_grad, where in parts:
        left, right = n[:, own_cols], n[:, other_cols]
        a = nt(left, lift_own[0]) + nt(right, lift_other[0])
        b = nt(left, lift_own[1]) + nt(right, lift_other[1])
        token_rows = pl.ds(pl.multiple_of(at * rows, rows), rows)
        dh = nt(cot[token_rows, own_cols], down_own[...])
        dh += nt(cot[token_rows, other_cols], down_other[...])
        cdf = 0.5 * (1.0 + lax.erf(a * (0.5**0.5)))
        act = a * cdf
        slope = cdf + a * jnp.exp(-0.5 * a * a) * (0.5 * 2.0**0.5 / jnp.pi**0.5)
        h = (act * b).astype(BF)
        da = (dh * b * slope).astype(BF)
        db = (dh * act).astype(BF)
        here = slice(where * rows, (where + 1) * rows)
        hidden[here, :] = h
        inner[here, :] = da
        gate[here, :] = db
        target[:, own_cols] = nn(h, down_own[...]).astype(target.dtype)
        target[:, other_cols] = nn(h, down_other[...]).astype(target.dtype)
        target_grad[:, own_cols] = (nn(da, lift_own[0]) + nn(db, lift_own[1])).astype(
            target_grad.dtype
        )
        target_grad[:, other_cols] = (nn(da, lift_other[0]) + nn(db, lift_other[1])).astype(
            target_grad.dtype
        )


def norm_back(v, gain, grad):
    center = v - jnp.mean(v, axis=-1, keepdims=True)
    spread = jnp.mean(center * center, axis=-1, keepdims=True)
    r = lax.rsqrt(spread + NORM_EPS)
    xhat = center * r
    eg = grad * gain
    mean_eg = jnp.mean(eg, axis=-1, keepdims=True)
    mean_egx = jnp.mean(eg * xhat, axis=-1, keepdims=True)
    back = r * (eg - mean_eg - xhat * mean_egx)
    return back, jnp.sum(grad * xhat, axis=0, keepdims=True)


def second_back_body(place, mine, theirs, middle, cot, gain, middle_grad, branch, gain_grad):
    grad = mine[...].astype(F32) + theirs[...].astype(F32)
    back, total = norm_back(middle[...], whole_gain(gain, place[2]), grad)
    result = cot[...].astype(F32) + back
    middle_grad[...] = result
    branch[...] = result.astype(BF)
    gain_grad[...] = total


def first_back_body(place, mine, theirs, x, middle_grad, gain, out, gain_grad):
    grad = mine[...].astype(F32) + theirs[...].astype(F32)
    back, total = norm_back(x[...].astype(F32), whole_gain(gain, place[2]), grad)
    out[...] = (middle_grad[...] + back).astype(BF)
    gain_grad[...] = total


def mix_back_body(place, b_own, b_other, w_own, w_other, o0, o1, o2, o3, branch, product):
    z, c, xi = place[0], place[1], place[2]
    rows = b_own.shape[0]
    half = w_own.shape[1]
    size = o0.shape[0]
    branch[pl.ds(pl.multiple_of(c * rows, rows), rows), :] = b_own[...]
    branch[pl.ds(pl.multiple_of((1 - c) * rows, rows), rows), :] = b_other[...]
    own_cols = pl.ds(pl.multiple_of(xi * half, half), half)
    other_cols = pl.ds(pl.multiple_of((1 - xi) * half, half), half)
    total = nt(w_own[...], branch[:, own_cols]) + nt(w_other[...], branch[:, other_cols])
    product[...] = total.astype(BF)
    for m, o in enumerate((o0, o1, o2, o3)):
        o[...] = product[pl.ds(pl.multiple_of((z ^ m) * size, size), size), :]


def project_back_body(place, d0, d1, d2, d3, w_own, w_other, keep, send, stacked):
    z, c, xi = place[0], place[1], place[2]
    width = w_own.shape[1]
    half = w_own.shape[2]
    size = d0.shape[0] // 3
    rows = keep.shape[0]
    for m, d in enumerate((d0, d1, d2, d3)):
        for kind in range(3):
            at = pl.ds(pl.multiple_of(kind * width + (z ^ m) * size, size), size)
            stacked[at, :] = d[kind * size : (kind + 1) * size, :]
    for target, at in ((keep, c), (send, 1 - c)):
        tokens = stacked[:, pl.ds(pl.multiple_of(at * rows, rows), rows)].T
        for w, hi in ((w_own, xi), (w_other, 1 - xi)):
            cols = pl.ds(pl.multiple_of(hi * half, half), half)
            weights = w[...].reshape(3 * width, half)
            target[:, cols] = nn(tokens, weights).astype(target.dtype)


def on_device(
    inputs,
    cotangent,
    lengths,
    attention_gain,
    triple_weight,
    mixing_weight,
    feedforward_gain,
    lifting_weight,
    down_weight,
    sizes,
):
    pairs = sizes["fsdp"] == 2
    sequences, span, width = inputs.shape
    half = width // 2
    heads_width = triple_weight.shape[2]
    size = width // H
    heads = heads_width // size
    units = down_weight.shape[0]
    z = lax.axis_index("ctx")
    core = lax.axis_index("tp") % 2
    xi = lax.axis_index("fsdp") if pairs else jnp.int32(0)
    place = jnp.stack([z, core, xi, xi]).astype(jnp.int32)
    quarter = span // 2

    def gather(array, axis):
        if pairs:
            return array, swap(array, "fsdp", 2, 1)
        full = lax.all_gather(array, "fsdp", axis=axis, tiled=True)
        return lax.split(full, [full.shape[axis] // 2] * 2, axis=axis)

    def scatter(full, axis):
        if not pairs:
            return lax.psum_scatter(
                full.astype(BF), "fsdp", scatter_dimension=axis, tiled=True
            ).astype(F32)
        n = full.shape[axis] // 2
        send = lax.dynamic_slice_in_dim(full, (1 - xi) * n, n, axis).astype(BF)
        keep = lax.dynamic_slice_in_dim(full, xi * n, n, axis)
        return keep + swap(send, "fsdp", 2, 1).astype(F32)

    def over_ctx(array):
        n = array.shape[1] // 2
        low, high = z % 2, z // 2
        send = lax.dynamic_slice_in_dim(array, (1 - low) * n, n, 1).astype(BF)
        keep = lax.dynamic_slice_in_dim(array, low * n, n, 1)
        keep = keep + swap(send, "ctx", 4, 1).astype(F32)
        n //= 2
        send = lax.dynamic_slice_in_dim(keep, (1 - high) * n, n, 1).astype(BF)
        keep = lax.dynamic_slice_in_dim(keep, high * n, n, 1)
        mine = (keep + swap(send, "ctx", 4, 2).astype(F32)).astype(BF)
        theirs = swap(mine, "ctx", 4, 2)
        pair = jnp.where(
            high == 0,
            jnp.concatenate([mine, theirs], axis=1),
            jnp.concatenate([theirs, mine], axis=1),
        )
        others = swap(pair, "ctx", 4, 1)
        return jnp.where(
            low == 0,
            jnp.concatenate([pair, others], axis=1),
            jnp.concatenate([others, pair], axis=1),
        ).astype(F32)

    def own_rows(array, s):
        return lax.dynamic_slice_in_dim(array[s], core * quarter, quarter, 0)

    gains = jnp.stack([attention_gain, feedforward_gain])
    gains_own, gains_other = gather(gains, 1)
    first_gain = jnp.stack([gains_own[0], gains_other[0]])
    second_gain = jnp.stack([gains_own[1], gains_other[1]])
    triple_t = triple_weight.transpose(1, 2, 0)
    shards = [gather(triple_t[kind], 1) for kind in (1, 0, 2)]
    key_w, query_w, value_w = shards
    mixing_w = gather(mixing_weight, 1)
    lifting_w = gather(lifting_weight.transpose(1, 2, 0), 2)
    down_w = gather(down_weight, 1)

    full_length = span * sizes["ctx"]
    frequency = ROPE_BASE ** (-2.0 * jnp.arange(size // 2, dtype=F32) / size)
    angles = frequency[:, None] * jnp.arange(full_length, dtype=jnp.int32).astype(F32)[None, :]
    cosine, sine = jnp.cos(angles), jnp.sin(angles)
    cosine_here = lax.dynamic_slice_in_dim(cosine, z * span, span, 1)
    sine_here = lax.dynamic_slice_in_dim(sine, z * span, span, 1)

    tokens = sequences * span
    (normed_first,) = kernel(
        norm_body,
        [place],
        [inputs.reshape(tokens, width), first_gain[0:1], first_gain[1:2]],
        [((tokens, width), BF)],
        name="norm_first",
    )

    def project(weights, rotated):
        tables = [cosine_here, sine_here] if rotated else []
        pieces = kernel(
            functools.partial(project_body, rotated),
            [place],
            [normed_first, *weights, *tables],
            [((size, tokens), BF)] * heads,
            scratch=[pltpu.VMEM((heads, size, tokens), BF)],
            flops=2 * tokens * width * heads_width,
            name="project",
        )
        return redistribute(pieces)

    def redistribute(pieces):
        return [pieces[0]] + [swap(pieces[m], "ctx", 4, m) for m in (1, 2, 3)]

    keys = project(key_w, True)
    queries = project(query_w, True)
    values = project(value_w, False)

    def attend(s):
        attention_flops = 4 * full_length * full_length * size
        *o, o_full, lse = kernel(
            functools.partial(attend_body, s, span),
            [place, lengths],
            [*queries, *keys, *values],
            [((size, span), BF)] * 4 + [((4, size, span), F32), ((4, span), F32)],
            scratch=[
                pltpu.VMEM((4, span, size), BF),
                pltpu.VMEM((4, size, span), BF),
                pltpu.VMEM((4, span), F32),
                pltpu.VMEM((4, span), F32),
            ],
            flops=4 * attention_flops,
            name="attend",
        )
        return redistribute(o), o_full, lse

    def across_row(keep, got):
        mine = (keep + got.astype(F32)).astype(BF)
        return mine, swap(mine, "tp", 4, ROW)

    middles, normed, mixtures, saved, feeds = [], [], [], [], []
    for s in range(sequences):
        o, o_full, lse = attend(s)
        saved.append((o_full, lse))
        keep, send, mixed = kernel(
            mix_body,
            [place],
            [*o, *mixing_w],
            [((quarter, width), F32), ((quarter, width), BF), ((heads_width, span), BF)],
            flops=2 * span * width * heads_width,
            name="mix",
        )
        mixtures.append(mixed)
        mine, theirs = across_row(keep, swap(send, "tp", 4, CORE))
        middle, n_own = kernel(
            second_norm_body,
            [place],
            [mine, theirs, own_rows(inputs, s), second_gain],
            [((quarter, width), F32), ((quarter, width), BF)],
            name="norm_second",
        )
        middles.append(middle)
        normed.append((n_own, swap(n_own, "tp", 4, CORE)))

    branches, middle_grads, gain_second_parts, grads_mixture, outs_mine = [], [], [], [], []
    for s in range(sequences):
        feed = kernel(
            feed_body,
            [place],
            [*normed[s], cotangent[s], *lifting_w, *down_w],
            [
                ((quarter, width), F32),
                ((quarter, width), BF),
                ((quarter, width), F32),
                ((quarter, width), BF),
                ((span, units), BF),
                ((span, units), BF),
                ((span, units), BF),
            ],
            flops=18 * span * width * units // 2 * 2,
            name="feed",
        )
        feeds.append(feed)
        mine, theirs = across_row(feed[2], swap(feed[3], "tp", 4, CORE))
        middle_grad, branch, gain_part = kernel(
            second_back_body,
            [place],
            [mine, theirs, middles[s], own_rows(cotangent, s), second_gain],
            [((quarter, width), F32), ((quarter, width), BF), ((1, width), F32)],
            name="norm_second_back",
        )
        middle_grads.append(middle_grad)
        gain_second_parts.append(gain_part)
        b_other = swap(branch, "tp", 4, CORE)
        *pieces, whole_branch = kernel(
            mix_back_body,
            [place],
            [branch, b_other, *mixing_w],
            [((size, span), BF)] * 4 + [((span, width), BF)],
            scratch=[pltpu.VMEM((heads_width, span), BF)],
            flops=2 * span * width * heads_width,
            name="mix_back",
        )
        branches.append(whole_branch)
        grads_mixture.append(redistribute(pieces))

    outs_mine = [
        (feeds[s][0] + swap(feeds[s][1], "tp", 4, CORE).astype(F32)).astype(BF)
        for s in range(sequences)
    ]
    stacked_out = jnp.stack(outs_mine)
    theirs_out = swap(stacked_out, "tp", 4, ROW)
    out_own = (
        jnp.stack(middles) + (stacked_out.astype(F32) + theirs_out.astype(F32))
    ).astype(BF)

    def both_cores(own):
        other = swap(own, "tp", 4, CORE)
        return jnp.where(
            core == 0,
            jnp.concatenate([own, other], axis=1),
            jnp.concatenate([other, own], axis=1),
        )

    output = both_cores(out_own)

    def token_sum(left, right):
        return lax.dot_general(left, right, (((0,), (0,)), ((), ())), preferred_element_type=F32)

    cot_ordered = [
        jnp.concatenate(
            [
                own_rows(cotangent, s),
                lax.dynamic_slice_in_dim(cotangent[s], (1 - core) * quarter, quarter, 0),
            ]
        )
        for s in range(sequences)
    ]
    cot_all = jnp.concatenate(cot_ordered)
    hidden_all = jnp.concatenate([f[4] for f in feeds])
    inner_all = jnp.concatenate([f[5] for f in feeds])
    gate_all = jnp.concatenate([f[6] for f in feeds])
    normed_all = jnp.concatenate([n for both in normed for n in both])
    down_gradient = over_ctx(scatter(token_sum(hidden_all, cot_all), 1))
    lifted_all = jnp.concatenate([inner_all, gate_all], axis=1)
    lifting_gradient = over_ctx(scatter(token_sum(lifted_all, normed_all), 1))
    mixing_gradient = over_ctx(
        scatter(
            nn(jnp.concatenate(mixtures, axis=1), jnp.concatenate(branches)),
            1,
        )
    )

    triple_own = jnp.stack([query_w[0], key_w[0], value_w[0]])
    triple_other = jnp.stack([query_w[1], key_w[1], value_w[1]])
    stacks, inputs_own, gain_first_parts = [], [], []
    for s in range(sequences):
        pieces = kernel(
            functools.partial(attend_back_body, s, span),
            [place, lengths],
            [*queries, *keys, *values, *grads_mixture[s], *saved[s], cosine, sine],
            [((3 * size, span), BF)] * 4,
            scratch=[
                pltpu.VMEM((4, span, size), BF),
                pltpu.VMEM((4, size, span), BF),
                pltpu.VMEM((4, span, size), BF),
                pltpu.VMEM((4, size, span), F32),
                pltpu.VMEM((4, span, size), F32),
                pltpu.VMEM((4, span, size), F32),
                pltpu.VMEM((4, span, size), BF),
                pltpu.VMEM((4, span, size), BF),
                pltpu.VMEM((4, span), F32),
            ],
            flops=40 * full_length * full_length * size,
            name="attend_back",
        )
        d = redistribute(pieces)
        keep, send, stacked = kernel(
            project_back_body,
            [place],
            [*d, triple_own, triple_other],
            [((quarter, width), F32), ((quarter, width), BF), ((3 * heads_width, span), BF)],
            flops=6 * span * width * heads_width,
            name="project_back",
        )
        stacks.append(stacked)
        mine, theirs = across_row(keep, swap(send, "tp", 4, CORE))
        own, gain_part = kernel(
            first_back_body,
            [place],
            [mine, theirs, own_rows(inputs, s), middle_grads[s], first_gain],
            [((quarter, width), BF), ((1, width), F32)],
            name="norm_first_back",
        )
        inputs_own.append(own)
        gain_first_parts.append(gain_part)
    input_gradient = both_cores(jnp.stack(inputs_own))

    triple_gradient = over_ctx(scatter(nn(jnp.concatenate(stacks, axis=1), normed_first), 1))

    gain_parts = jnp.concatenate(
        [
            gain_first_parts[0] + gain_first_parts[1],
            gain_second_parts[0] + gain_second_parts[1],
        ]
    )
    gain_parts = gain_parts + swap(gain_parts, "tp", 4, CORE)
    gain_parts = scatter(gain_parts, 1)
    gain_parts = gain_parts + swap(gain_parts, "ctx", 4, 1)
    gain_parts = gain_parts + swap(gain_parts, "ctx", 4, 2)

    return (
        output,
        input_gradient,
        gain_parts[0],
        triple_gradient.reshape(3, heads_width, -1).transpose(2, 0, 1),
        mixing_gradient,
        gain_parts[1],
        lifting_gradient.reshape(2, units, -1).transpose(2, 0, 1),
        down_gradient,
    )


def solution(mesh):
    in_specs = (
        P("fsdp", "ctx", None),
        P("fsdp", "ctx", None),
        P("fsdp"),
        P("fsdp"),
        P("fsdp", None, "tp"),
        P("tp", "fsdp"),
        P("fsdp"),
        P("fsdp", None, "tp"),
        P("tp", "fsdp"),
    )
    out_specs = (
        P("fsdp", "ctx", None),
        P("fsdp", "ctx", None),
        P("fsdp"),
        P("fsdp", None, "tp"),
        P("tp", "fsdp"),
        P("fsdp"),
        P("fsdp", None, "tp"),
        P("tp", "fsdp"),
    )
    return jax.shard_map(
        functools.partial(on_device, sizes=dict(mesh.shape)),
        mesh=mesh,
        in_specs=in_specs,
        out_specs=out_specs,
        check_vma=False,
    )
```

```python
import functools

import jax
import jax.numpy as jnp
from jax import lax
from jax.experimental import pallas as pl
from jax.experimental.pallas import tpu as pltpu
from jax.sharding import PartitionSpec as P

H = 16
NORM_EPS = 1e-05
ROPE_BASE = 160000.0
MASKED = -1e30
BF = jnp.bfloat16
F32 = jnp.float32
FLOPS_PER_US = 1153e6
CORE, ROW = 1, 2


def nn(a, b):
    return lax.dot_general(a, b, (((1,), (0,)), ((), ())), preferred_element_type=F32)


def nt(a, b):
    return lax.dot_general(a, b, (((1,), (1,)), ((), ())), preferred_element_type=F32)


def tn(a, b):
    return lax.dot_general(a, b, (((0,), (0,)), ((), ())), preferred_element_type=F32)


def swap(array, axis, size, step):
    return lax.ppermute(array, axis, [(i, i ^ step) for i in range(size)])


def part(start, size):
    return pl.ds(pl.multiple_of(start * size, size), size)


def piece(refs, z, m):
    return refs[m] if len(refs) == 4 else refs[0].at[z ^ m]


class Part:
    def __init__(self, array, index):
        self.array, self.index = array, index


class Sequence:
    def __init__(self):
        self.last = None

    def __call__(self, body, scalars, arrays, outs, scratch=(), us=1, name=None, wait=(), mib=16):
        operands = [a.array if isinstance(a, Part) else a for a in arrays]
        specs = [pl.BlockSpec(memory_space=pltpu.VMEM)] * len(arrays)
        after = list(wait) + ([] if self.last is None else [self.last])
        first = len(scalars) + len(arrays)

        def run(*refs):
            taken = refs[len(scalars) : first]
            taken = [
                r.at[a.index] if isinstance(a, Part) else r
                for r, a in zip(taken, arrays, strict=True)
            ]
            body(*refs[: len(scalars)], *taken, *refs[first + len(after) :])

        results = pl.pallas_call(
            run,
            out_shape=[jax.ShapeDtypeStruct(s, t) for s, t in outs],
            in_specs=[pl.BlockSpec(memory_space=pltpu.SMEM)] * len(scalars)
            + specs
            + [pl.BlockSpec(memory_space=pl.ANY)] * len(after),
            out_specs=[pl.BlockSpec(memory_space=pltpu.VMEM)] * len(outs),
            scratch_shapes=list(scratch),
            compiler_params=pltpu.CompilerParams(vmem_limit_bytes=mib << 20),
            cost_estimate=pl.CostEstimate(
                flops=int(us * FLOPS_PER_US), bytes_accessed=0, transcendentals=0
            ),
            name=name,
        )(*scalars, *operands, *after)
        self.last = min(results, key=lambda r: r.size)
        return results


def whole_gain(gain, xi):
    own, other = gain[0:1, :].astype(F32), gain[1:2, :].astype(F32)
    low = jnp.where(xi == 0, own, other)
    high = jnp.where(xi == 0, other, own)
    return jnp.concatenate([low, high], axis=1)


def norm_body(place, x, gain, out):
    gain_row = whole_gain(gain, place[2])
    step = 256
    for s in range(x.shape[0]):

        def block(i, carry, s=s):
            at = part(i, step)
            v = x[s, at, :].astype(F32)
            center = v - jnp.mean(v, axis=-1, keepdims=True)
            spread = jnp.mean(center * center, axis=-1, keepdims=True)
            out[s, at, :] = (center * lax.rsqrt(spread + NORM_EPS) * gain_row).astype(BF)
            return carry

        lax.fori_loop(0, x.shape[1] // step, block, 0)


def project_body(size, kinds, place, *refs):
    normed, cosine, sine = refs[0:3]
    weights = refs[3 : 3 + 2 * len(kinds)]
    outs, heads = refs[3 + 2 * len(kinds) : -1], refs[-1]
    count = len(outs)
    half = weights[0].shape[0]
    z, xi = place[0], place[2]
    blocks = normed.shape[0] if len(normed.shape) == 3 else 1
    span = normed.shape[-2]
    for s in range(blocks):
        rows = slice(s * span, (s + 1) * span)
        source = normed.at[s] if len(normed.shape) == 3 else normed
        n_own = source[:, part(xi, half)]
        n_other = source[:, part(1 - xi, half)]
        for i, rotated in enumerate(kinds):
            acc = nt(weights[2 * i][...].T, n_own) + nt(weights[2 * i + 1][...].T, n_other)
            for h in range(count):
                u = acc[h * size : (h + 1) * size]
                if rotated:
                    u1, u2 = u[: size // 2], u[size // 2 :]
                    co, si = cosine[...], sine[...]
                    u = jnp.concatenate([u1 * co - u2 * si, u2 * co + u1 * si], axis=0)
                heads[h, i * size : (i + 1) * size, rows] = u.astype(BF)
    for m in range(count):
        outs[m][...] = heads[z ^ m]


def attend_body(s, span, place, lengths, *refs):
    k, qv = refs[0:4], refs[4:8]
    *o, o_full, lse, keys, values, top, total = refs[8:]
    z = place[0]
    size = k[0].shape[0]
    cols = slice(s * span, (s + 1) * span)
    for m in range(4):
        keys[z ^ m] = k[m][:, cols].T
        values[z ^ m] = qv[m][size:, :]
    top[...] = jnp.full_like(top, MASKED)
    total[...] = jnp.zeros_like(total)
    o_full[...] = jnp.zeros_like(o_full)
    length = lengths[s]
    full = length // span
    rest = length - full * span

    def step(j, limit):
        key, value = keys[j], values[j]
        for m in range(4):
            st = nn(key, qv[m][:size, :]) * (size**-0.5)
            if limit is not None:
                st = jnp.where(lax.broadcasted_iota(jnp.int32, st.shape, 0) < limit, st, MASKED)
            before = top[m : m + 1, :]
            peak = jnp.maximum(before, jnp.max(st, axis=0, keepdims=True))
            p = jnp.exp(st - peak)
            scale = jnp.exp(before - peak)
            top[m : m + 1, :] = peak
            total[m : m + 1, :] = total[m : m + 1, :] * scale + jnp.sum(p, axis=0, keepdims=True)
            o_full[m] = o_full[m] * scale + nn(value, p.astype(BF))

    def whole(j, carry):
        step(j, None)
        return carry

    lax.fori_loop(0, full, whole, 0)

    @pl.when(rest > 0)
    def _():
        step(full, rest)

    for m in range(4):
        result = o_full[m] / total[m : m + 1, :]
        o_full[m] = result
        piece(o, z, m)[...] = result.astype(BF)
        lse[m : m + 1, :] = top[m : m + 1, :] + jnp.log(total[m : m + 1, :])


def attend_back_body(s, span, place, lengths, *refs):
    k, qv = refs[0:4], refs[4:8]
    keys, keys_t, values, d_query, d_key, d_value, queries, grads, delta = refs[-9:]
    count = (len(refs) - 21) // 2
    do, out = refs[8 : 8 + count], refs[12 + count : -9]
    o_full, lse, cosine, sine = refs[8 + count : 12 + count]
    z = place[0]
    size = k[0].shape[0]
    cols = slice(s * span, (s + 1) * span)
    for m in range(4):
        keys[z ^ m] = k[m][:, cols].T
        keys_t[z ^ m] = k[m][:, cols]
        values[z ^ m] = qv[m][size:, :].T
        queries[m] = qv[m][:size, :].T
        grads[m] = piece(do, z, m)[...].T
        delta[m : m + 1, :] = jnp.sum(piece(do, z, m)[...].astype(F32) * o_full[m], axis=0, keepdims=True)
    d_query[...] = jnp.zeros_like(d_query)
    d_key[...] = jnp.zeros_like(d_key)
    d_value[...] = jnp.zeros_like(d_value)
    length = lengths[s]
    full = length // span
    rest = length - full * span
    factor = size**-0.5

    def step(j, limit):
        key, key_t, value = keys[j], keys_t[j], values[j]
        for m in range(4):
            st = nn(key, qv[m][:size, :]) * factor
            if limit is not None:
                st = jnp.where(lax.broadcasted_iota(jnp.int32, st.shape, 0) < limit, st, MASKED)
            p = jnp.exp(st - lse[m : m + 1, :])
            dp = nn(value, piece(do, z, m)[...])
            ds = (p * (dp - delta[m : m + 1, :]) * factor).astype(BF)
            d_value[j] += nn(p.astype(BF), grads[m])
            d_key[j] += nn(ds, queries[m])
            d_query[m] += nn(key_t, ds)

    def whole(j, carry):
        step(j, None)
        return carry

    lax.fori_loop(0, full, whole, 0)

    @pl.when(rest > 0)
    def _():
        step(full, rest)

    def back(w, j):
        at = part(j, span)
        co, si = cosine[:, at], sine[:, at]
        w1, w2 = w[: size // 2], w[size // 2 :]
        return jnp.concatenate([w1 * co + w2 * si, w2 * co - w1 * si], axis=0).astype(BF)

    for m in range(4):
        j = z ^ m
        target = piece(out, z, m)
        target[0:size, :] = back(d_query[m], j)
        target[size : 2 * size, :] = back(d_key[j].T, j)
        target[2 * size :, :] = d_value[j].T.astype(BF)


def heads_body(place, *refs):
    *o, mixed = refs
    size = mixed.shape[0] // 4
    for m in range(4):
        mixed[part(place[0] ^ m, size), :] = piece(o, place[0], m)[...]


def mix_body(place, mixed, *refs):
    *weights, out = refs
    c, xi = place[1], place[2]
    width, half = weights[0].shape
    rows = out.shape[0]
    left = [mixed[part(at, width), part(c, rows)].T for at in (c, 1 - c)]
    for side, hi in ((0, xi), (1, 1 - xi)):
        total = nn(left[0], weights[side][...]) + nn(left[1], weights[2 + side][...])
        out[:, part(hi, half)] = total.astype(BF)


def add_body(a, b, out):
    out[...] = (a[...].astype(F32) + b[...].astype(F32)).astype(out.dtype)


def feed_body(place, mine, theirs, x, gain, cot, *refs):
    weights = refs[0:4]
    middle, out, out_grad, *packs = refs[4:]
    c, xi = place[1], place[2]
    rows, width = middle.shape
    half = width // 2
    units = weights[0].shape[0] // 3
    lanes = (packs[0].shape[1] - width) // 3
    token_rows = part(c, rows)
    v = x[token_rows, :].astype(F32) + (mine[...].astype(F32) + theirs[...].astype(F32))
    middle[...] = v
    center = v - jnp.mean(v, axis=-1, keepdims=True)
    spread = jnp.mean(center * center, axis=-1, keepdims=True)
    n = (center * lax.rsqrt(spread + NORM_EPS) * whole_gain(gain, place[2])).astype(BF)
    columns = (part(xi, half), part(1 - xi, half))
    packs[0][:, :width] = n
    packs[1][:, :width] = n
    totals, totals_grad = [None, None], [None, None]
    for i, pack in enumerate(packs):
        sides = weights[2 * i : 2 * i + 2]

        def over(left, rows_of, sides=sides):
            return sum(nt(left(cols), w[rows_of, :]) for w, cols in zip(sides, columns))

        inner, gate, down = (slice(k * units, (k + 1) * units) for k in range(3))
        a = over(lambda cols, pack=pack: pack[:, cols], inner)
        b = over(lambda cols, pack=pack: pack[:, cols], gate)
        dh = over(lambda cols: cot[token_rows, cols], down)
        cdf = 0.5 * (1.0 + lax.erf(a * (0.5**0.5)))
        act = a * cdf
        slope = cdf + a * jnp.exp(-0.5 * a * a) * (0.5 * 2.0**0.5 / jnp.pi**0.5)
        h = (act * b).astype(BF)
        da = (dh * b * slope).astype(BF)
        db = (dh * act).astype(BF)
        for k, value in enumerate((h, da, db)):
            pack[:, width + k * lanes : width + k * lanes + units] = value
        for side, w in enumerate(sides):
            term = nn(da, w[inner, :]) + nn(db, w[gate, :])
            totals_grad[side] = term if i == 0 else totals_grad[side] + term
            term = nn(h, w[down, :])
            totals[side] = term if i == 0 else totals[side] + term
    for side, cols in enumerate(columns):
        out_grad[:, cols] = totals_grad[side].astype(BF)
        out[:, cols] = totals[side].astype(BF)


def feed_grad_body(units, kinds, place, *refs):
    *packs, cot, keep, send = refs
    c, xi = place[1], place[2]
    half = keep.shape[1]
    rows, lanes = packs[0].shape
    lanes = (lanes - 2 * half) // 3
    for target, hi in ((send, 1 - xi), (keep, xi)):
        for row, kind in enumerate(kinds):
            total = None
            for i, pack in enumerate(packs):
                start = 2 * half + kind * lanes
                if kind == 0:
                    right = cot[i // 2, part(c if i % 2 == 0 else 1 - c, rows), part(hi, half)]
                else:
                    right = pack[:, part(hi, half)]
                term = tn(pack[:, start : start + units], right)
                total = term if total is None else total + term
            target[row * units : (row + 1) * units, :] = total.astype(target.dtype)


def attention_grad_body(place, *refs):
    stacks, (normed,), gains, mixed, branches = refs[0:2], refs[2:3], refs[3:7], refs[7:9], refs[9:13]
    keep, send = refs[13:]
    c, xi = place[1], place[2]
    half = keep.shape[1]
    rows = stacks[0].shape[0]
    width = rows // 3
    under = keep.shape[0] - rows - width
    tokens = branches[0].shape[0]
    for target, hi in ((send, 1 - xi), (keep, xi)):
        cols = part(hi, half)
        total = nn(stacks[0][...], normed[0, :, cols]) + nn(stacks[1][...], normed[1, :, cols])
        target[0:rows, :] = total.astype(target.dtype)
        first = gains[0][:, cols] + gains[1][:, cols]
        second = 0.5 * (gains[2][:, cols] + gains[3][:, cols])
        which = lax.broadcasted_iota(jnp.int32, (under, half), 0)
        both = jnp.where(which == 0, first, jnp.where(which == 1, second, 0.0))
        target[rows : rows + under, :] = both.astype(target.dtype)
        total = None
        for s in range(2):
            for side, at in ((0, c), (1, 1 - c)):
                left = mixed[s][part(c, width), part(at, tokens)]
                term = nn(left, branches[2 * s + side][:, cols])
                total = term if total is None else total + term
        target[rows + under :, :] = total.astype(target.dtype)


def halve_body(which, place, a, b, keep, send):
    columns = keep.shape[1]
    for target, at in ((send, 1 - place[which]), (keep, place[which])):
        cols = part(at, columns)
        total = a[:, cols].astype(F32) + b[:, cols].astype(F32)
        target[...] = total.astype(target.dtype)


def unite_body(which, place, mine, theirs, out):
    columns = mine.shape[1]
    out[:, part(place[which], columns)] = mine[...].astype(out.dtype)
    out[:, part(1 - place[which], columns)] = theirs[...].astype(out.dtype)


def lifting_end_body(which, place, mine, theirs, lifting):
    columns = mine.shape[1]
    units = lifting.shape[1]
    for part_of, at in ((mine, place[which]), (theirs, 1 - place[which])):
        for kind in range(2):
            value = part_of[kind * units : (kind + 1) * units, :]
            lifting[kind, :, part(at, columns)] = value.astype(F32)


def attention_end_body(which, place, mine, theirs, gains_mine, gains_theirs, triple, mixing, gains):
    columns = mine.shape[1]
    width = triple.shape[2]
    pairs = ((mine, gains_mine, place[which]), (theirs, gains_theirs, 1 - place[which]))
    for part_of, gains_of, at in pairs:
        cols = part(at, columns)
        for kind in range(3):
            value = part_of[kind * width : (kind + 1) * width, :]
            triple[kind, cols, :] = value.T.astype(F32)
        gains[:, cols] = gains_of[...]
        mixing[:, cols] = part_of[part_of.shape[0] - width :, :].astype(F32)


def norm_back(v, gain, grad):
    center = v - jnp.mean(v, axis=-1, keepdims=True)
    spread = jnp.mean(center * center, axis=-1, keepdims=True)
    r = lax.rsqrt(spread + NORM_EPS)
    xhat = center * r
    eg = grad * gain
    mean_eg = jnp.mean(eg, axis=-1, keepdims=True)
    mean_egx = jnp.mean(eg * xhat, axis=-1, keepdims=True)
    back = r * (eg - mean_eg - xhat * mean_egx)
    return back, jnp.sum(grad * xhat, axis=0, keepdims=True)


def second_back_body(place, mine, theirs, middle, cot, gain, *refs):
    *weights, middle_grad, branch, gain_grad, product = refs
    c, xi = place[1], place[2]
    rows = middle.shape[0]
    heads_width, half = weights[0].shape
    grad = mine[...].astype(F32) + theirs[...].astype(F32)
    back, total = norm_back(middle[...], whole_gain(gain, xi), grad)
    result = cot[part(c, rows), :].astype(F32) + back
    middle_grad[...] = result
    branch[...] = result.astype(BF)
    gain_grad[...] = total
    left, right = branch[:, part(xi, half)], branch[:, part(1 - xi, half)]
    for i, at in ((0, c), (1, 1 - c)):
        term = nt(weights[2 * i][...], left) + nt(weights[2 * i + 1][...], right)
        product[part(at, heads_width), :] = term.astype(BF)


def pieces_body(place, product, *outs):
    z, c = place[0], place[1]
    rows, columns = product.shape
    size = rows // 16
    for m in range(4):
        for k in range(2):
            rows_here = part(8 * k + 4 * c + (z ^ m), size)
            piece(outs, z, m)[:, k * columns : (k + 1) * columns] = product[rows_here, :]


def first_back_body(place, mine, theirs, x, middle_grad, gain, out):
    rows = middle_grad.shape[0]
    grad = mine[...].astype(F32) + theirs[...].astype(F32)
    back, _ = norm_back(x[part(place[1], rows), :].astype(F32), whole_gain(gain, place[2]), grad)
    out[...] = (middle_grad[...] + back).astype(BF)


def output_body(place, m0, m1, f0, f1, theirs, out):
    for s, (m, f) in enumerate(((m0, f0), (m1, f1))):
        out[s] = (m[...] + (f[...].astype(F32) + theirs[s].astype(F32))).astype(BF)


def join_body(place, *refs):
    *parts, out = refs
    rows = parts[0].shape[0]
    for s in range(len(parts) // 2):
        out[s, part(place[1], rows), :] = parts[2 * s][...]
        out[s, part(1 - place[1], rows), :] = parts[2 * s + 1][...]


def join_stacked_body(place, own, other, out):
    rows = own.shape[1]
    out[:, part(place[1], rows), :] = own[...]
    out[:, part(1 - place[1], rows), :] = other[...]


def project_back_body(place, *refs):
    *d, x = refs[:-10]
    weights, (keep, send, stacked, gain_grad) = refs[-10:-4], refs[-4:]
    c, rows = place[1], keep.shape[0]
    z, xi = place[0], place[2]
    half, width = weights[0].shape
    size = d[0].shape[-2] // 3
    for m in range(4):
        here = piece(d, z, m)
        for kind in range(3):
            at = part(kind * (width // size) + (z ^ m), size)
            stacked[at, :] = here[kind * size : (kind + 1) * size, :]
    for target, at in ((send, 1 - c), (keep, c)):
        tokens = stacked[:, part(at, rows)].T
        v = x[part(at, rows), :].astype(F32)
        mean = jnp.mean(v, axis=-1, keepdims=True)
        center = v - mean
        r = lax.rsqrt(jnp.mean(center * center, axis=-1, keepdims=True) + NORM_EPS)
        for side, hi in ((0, xi), (1, 1 - xi)):
            total = None
            for kind in range(3):
                term = nt(
                    tokens[:, kind * width : (kind + 1) * width], weights[2 * kind + side][...]
                )
                total = term if total is None else total + term
            cols = part(hi, half)
            target[:, cols] = total.astype(target.dtype)
            xhat = (x[part(at, rows), cols].astype(F32) - mean) * r
            sums = jnp.sum(total * xhat, axis=0, keepdims=True)
            if target is send:
                gain_grad[:, cols] = sums
            else:
                gain_grad[:, cols] += sums


def on_device(
    inputs,
    cotangent,
    lengths,
    attention_gain,
    triple_weight,
    mixing_weight,
    feedforward_gain,
    lifting_weight,
    down_weight,
    sizes,
):
    run = Sequence()
    pairs = sizes["fsdp"] == 2
    sequences, span, width = inputs.shape
    half = width // 2
    heads_width = triple_weight.shape[2]
    size = width // H
    heads = heads_width // size
    units = down_weight.shape[0]
    z = lax.axis_index("ctx")
    core = lax.axis_index("tp") % 2
    xi = lax.axis_index("fsdp") if pairs else jnp.int32(0)
    place = jnp.stack([z, core, xi, z % 2, z // 2]).astype(jnp.int32)
    quarter = span // 2
    both = range(sequences)

    def gather(array, axis):
        if pairs:
            return array, swap(array, "fsdp", 2, 1)
        full = lax.all_gather(array, "fsdp", axis=axis, tiled=True)
        return lax.split(full, [full.shape[axis] // 2] * 2, axis=axis)

    def over_fsdp(keep, send):
        if pairs:
            return keep, swap(send, "fsdp", 2, 1)
        full = jnp.concatenate([keep.astype(BF), send], axis=1)
        keep = lax.psum_scatter(full, "fsdp", scatter_dimension=1, tiled=True)
        return keep, jnp.zeros_like(keep)

    def added(a, b, kind, name):
        return run(add_body, [], [a, b], [(b.shape, kind)], name=name)[0]

    cores = [[0, 1], [2, 3]]

    def both_cores(array):
        return lax.all_gather(array, "tp", axis_index_groups=cores, axis=0, tiled=True)

    def redistribute(pieces):
        moved = {m: swap(pieces[m], "ctx", 4, m) for m in (2, 3, 1)}
        return [pieces[0], moved[1], moved[2], moved[3]]

    low, high = 3, 4

    class Reduction:
        def __init__(self, keep, send):
            self.a, self.b = over_fsdp(keep, send)
            if not pairs:
                self.a = lax.psum(self.a, "ctx").astype(F32)

        def halve(self, which, step):
            if not pairs:
                return
            rows, columns = self.a.shape
            shape = (rows, columns // 2)
            self.a, send = run(
                functools.partial(halve_body, which),
                [place],
                [self.a, self.b],
                [(shape, F32), (shape, BF)],
                us=1,
                name="halve",
            )
            self.b = swap(send, "ctx", 4, step)

        def unite(self, which, kind):
            if not pairs:
                return
            rows, columns = self.b.shape
            shape = (rows, columns * 2)
            (self.a,) = run(
                functools.partial(unite_body, which),
                [place],
                [self.a, self.b],
                [(shape, kind)],
                us=0.7,
                name="unite",
            )

        def first(self):
            self.halve(low, 1)

        def second(self):
            self.halve(high, 2)

        def third(self):
            if not pairs:
                return
            (self.a,) = run(
                add_body, [], [self.a, self.b], [(self.b.shape, BF)], us=0.4, name="sum_ctx"
            )
            self.b = swap(self.a, "ctx", 4, 2)

        def fourth(self):
            if not pairs:
                return
            self.unite(high, BF)
            self.b = swap(self.a, "ctx", 4, 1)

        def last(self, body, outs, name, more=()):
            return run(
                functools.partial(body, low), [place], [self.a, self.b, *more], outs, us=2, name=name
            )

    key_w = gather(triple_weight[:, 1], 0)
    gains_own, gains_other = gather(jnp.stack([attention_gain, feedforward_gain]), 1)
    first_gain = jnp.stack([gains_own[0], gains_other[0]])
    second_gain = jnp.stack([gains_own[1], gains_other[1]])

    full_length = span * sizes["ctx"]
    frequency = ROPE_BASE ** (-2.0 * jnp.arange(size // 2, dtype=F32) / size)
    angles = frequency[:, None] * jnp.arange(full_length, dtype=jnp.int32).astype(F32)[None, :]
    cosine, sine = jnp.cos(angles), jnp.sin(angles)
    cosine_here = lax.dynamic_slice_in_dim(cosine, z * span, span, 1)
    sine_here = lax.dynamic_slice_in_dim(sine, z * span, span, 1)

    (normed_first,) = run(
        norm_body, [place], [inputs, first_gain], [(inputs.shape, BF)], name="norm_first"
    )

    def later(array):
        return lax.optimization_barrier((array, run.last))[0]

    query_w = gather(later(triple_weight[:, 0]), 0)
    value_w = gather(later(triple_weight[:, 2]), 0)

    def project(normed, kinds, weights, columns, wait=()):
        return redistribute(
            run(
                functools.partial(project_body, size, kinds),
                [place],
                [normed, cosine_here, sine_here, *weights],
                [((len(kinds) * size, columns), BF)] * heads,
                scratch=[pltpu.VMEM((heads, len(kinds) * size, columns), BF)],
                us=1.3,
                wait=wait,
                name="project",
            )
        )

    keys = project(normed_first, (True,), key_w, sequences * span)
    feed_own = jnp.concatenate(
        [lifting_weight[:, 0].T, lifting_weight[:, 1].T, down_weight], axis=0
    )
    first, second = Part(normed_first, 0), Part(normed_first, 1)
    mixing_w = gather(later(mixing_weight), 1)
    rest = [project(first, (True, False), (*query_w, *value_w), span, keys[1:3])]
    feed_w = gather(later(feed_own), 1)
    waits = [keys[3], rest[0][1], mixing_w[1]]
    rest.append(project(second, (True, False), (*query_w, *value_w), span, waits))

    attended = []

    def attend(s, wait):
        *o, o_full, lse = run(
            functools.partial(attend_body, s, span),
            [place, lengths],
            [*keys, *rest[s]],
            [*[((size, span), BF)] * 4, ((4, size, span), F32), ((4, span), F32)],
            scratch=[
                pltpu.VMEM((4, span, size), BF),
                pltpu.VMEM((4, size, span), BF),
                pltpu.VMEM((4, span), F32),
                pltpu.VMEM((4, span), F32),
            ],
            us=10,
            wait=wait,
            name="attend",
        )
        attended.append((redistribute(o), o_full, lse))

    attend(0, [])
    attend(1, [])

    mixtures, sums, mixing_all = [], [], list(mixing_w)

    def mix(s, wait):
        (mixed,) = run(
            heads_body,
            [place],
            attended[s][0],
            [((heads_width, span), BF)],
            us=0.6,
            wait=wait,
            name="heads",
        )
        if s == 0:
            mixing_all.extend(swap(later(w), "tp", 4, CORE) for w in mixing_w)
        mixed = both_cores(mixed)
        mixtures.append(mixed)
        (mine,) = run(
            mix_body, [place], [mixed, *mixing_all], [((quarter, width), BF)], us=1, name="mix"
        )
        sums.append((mine, swap(mine, "tp", 4, ROW)))

    mix(0, [])
    feed_theirs = [swap(later(w), "tp", 4, CORE) for w in feed_w]
    mix(1, [])

    feeds, grads, packs = [], [], []
    lanes = -(-units // 128) * 128
    for s in both:
        feed = run(
            feed_body,
            [place],
            [*sums[s], Part(inputs, s), second_gain, Part(cotangent, s), *feed_w, *feed_theirs],
            [
                ((quarter, width), F32),
                ((quarter, width), BF),
                ((quarter, width), BF),
                ((quarter, width + 3 * lanes), BF),
                ((quarter, width + 3 * lanes), BF),
            ],
            us=6.6,
            name="feed",
        )
        feeds.append(feed)
        grads.append((feed[2], swap(feed[2], "tp", 4, ROW)))
        packs.append((feed[3], feed[4]))
    branches, middle_grads, gain_second, mixture_grads = [], [], [], []

    def second_back(s, exchange=None, between=None):
        middle_grad, branch, gain_part, product = run(
            second_back_body,
            [place],
            [*grads[s], feeds[s][0], Part(cotangent, s), second_gain, *mixing_all],
            [
                ((quarter, width), F32),
                ((quarter, width), BF),
                ((1, width), F32),
                ((2 * heads_width, quarter), BF),
            ],
            us=2,
            name="norm_second_back",
        )
        middle_grads.append(middle_grad)
        gain_second.append(gain_part)
        branches.append(branch)
        if exchange is not None:
            exchange()
        pieces = run(
            pieces_body,
            [place],
            [both_cores(product)],
            [((size, span), BF)] * 4,
            us=0.6,
            name="pieces",
        )
        mixture_grads.append(redistribute(pieces))
        if between is not None:
            between()

    reductions, exchanged = [], []

    def exchange_packs():
        for mine, theirs in packs:
            exchanged.extend([mine, swap(later(theirs), "tp", 4, CORE)])

    def start_feed_grad(kinds):
        rows = len(kinds) * units
        reductions.append(
            Reduction(
                *run(
                    functools.partial(feed_grad_body, units, kinds),
                    [place],
                    [*exchanged, cotangent],
                    [((rows, half), F32), ((rows, half), BF)],
                    us=1.7 * len(kinds),
                    name="feed_grad",
                )
            )
        )

    second_back(0, exchange_packs, lambda: start_feed_grad((1, 2)))
    second_back(1)

    def attend_back(s, wait):
        _, o_full, lse = attended[s]
        return redistribute(
            run(
                functools.partial(attend_back_body, s, span),
                [place, lengths],
                [*keys, *rest[s], *mixture_grads[s], o_full, lse, cosine, sine],
                [((3 * size, span), BF)] * 4,
                scratch=[
                    pltpu.VMEM((4, span, size), BF),
                    pltpu.VMEM((4, size, span), BF),
                    pltpu.VMEM((4, span, size), BF),
                    pltpu.VMEM((4, size, span), F32),
                    pltpu.VMEM((4, span, size), F32),
                    pltpu.VMEM((4, span, size), F32),
                    pltpu.VMEM((4, span, size), BF),
                    pltpu.VMEM((4, span, size), BF),
                    pltpu.VMEM((4, span), F32),
                ],
                us=13,
                wait=wait,
                name="attend_back",
            )
        )

    d = [attend_back(0, [])]
    start_feed_grad((0,))
    lifting_grad, down_grad = reductions
    d.append(attend_back(1, []))

    stacks, gain_first, back_sums = [], [], []

    def project_back(s):
        keep, send, stacked, gain_part = run(
            project_back_body,
            [place],
            [*d[s], Part(inputs, s), *query_w, *key_w, *value_w],
            [
                ((quarter, width), F32),
                ((quarter, width), BF),
                ((3 * heads_width, span), BF),
                ((1, width), F32),
            ],
            us=2.4,
            name="project_back",
        )
        stacks.append(stacked)
        gain_first.append(gain_part)
        return keep, swap(send, "tp", 4, CORE)

    def project_sum(keep, got):
        (mine,) = run(
            add_body, [], [keep, got], [((quarter, width), BF)], us=0.4, name="project_sum"
        )
        back_sums.append((mine, swap(mine, "tp", 4, ROW)))

    def first_back(s):
        (own,) = run(
            first_back_body,
            [place],
            [*back_sums[s], Part(inputs, s), middle_grads[s], first_gain],
            [((quarter, width), BF)],
            us=1.3,
            name="norm_first_back",
        )
        return own, swap(own, "tp", 4, CORE)

    lifting_grad.first()
    partial = project_back(0)
    down_grad.first()
    project_sum(*partial)
    lifting_grad.second()
    partial = project_back(1)
    branches = [b for mine in branches for b in (mine, swap(later(mine), "tp", 4, CORE))]
    inputs_own = list(first_back(0))
    rows = 3 * heads_width
    total_rows = rows + 16 + heads_width
    attention_grad = Reduction(
        *run(
            attention_grad_body,
            [place],
            [*stacks, normed_first, *gain_first, *gain_second, *mixtures, *branches],
            [((total_rows, half), F32), ((total_rows, half), BF)],
            us=4.5,
            name="attention_grad",
        )
    )
    project_sum(*partial)
    out_theirs = swap(later(jnp.stack([f[1] for f in feeds])), "tp", 4, ROW)

    down_grad.second()
    lifting_grad.third()
    inputs_own += first_back(1)
    down_grad.third()
    attention_grad.first()
    lifting_grad.fourth()
    (input_gradient,) = run(
        join_body, [place], inputs_own, [(inputs.shape, BF)], name="gradient_join"
    )
    down_grad.fourth()
    attention_grad.second()
    (out_own,) = run(
        output_body,
        [place],
        [*[f[0] for f in feeds], *[f[1] for f in feeds], out_theirs],
        [((sequences, quarter, width), BF)],
        name="output",
    )
    out_other = swap(out_own, "tp", 4, CORE)
    if pairs:
        (lifting_gradient,) = lifting_grad.last(
            lifting_end_body, [((2, units, half), F32)], "lifting_end"
        )
    else:
        lifting_gradient = lifting_grad.a.reshape(2, units, -1)
    attention_grad.third()
    down_grad.unite(low, F32)
    (output,) = run(
        join_stacked_body, [place], [out_own, out_other], [(inputs.shape, BF)], name="output_join"
    )
    attention_grad.fourth()
    if pairs:
        gains_half = jnp.sum(
            lax.all_gather(attention_grad.a[rows : rows + 2].astype(F32), "tp"), axis=0
        )
        gains_other = swap(gains_half, "ctx", 4, 1)
        triple_gradient, mixing_gradient, gain_parts = attention_grad.last(
            attention_end_body,
            [((3, half, heads_width), F32), ((heads_width, half), F32), ((2, half), F32)],
            "attention_end",
            [gains_half, gains_other],
        )
    else:
        total = attention_grad.a
        gain_parts = jnp.sum(lax.all_gather(total[rows : rows + 2], "tp"), axis=0)
        triple_gradient = total[:rows].reshape(3, heads_width, -1).transpose(0, 2, 1)
        mixing_gradient = total[rows + 16 :]
    down_gradient = down_grad.a
    lifting_gradient = lifting_gradient.transpose(2, 0, 1)
    triple_gradient = triple_gradient.transpose(1, 0, 2)

    return (
        output,
        input_gradient,
        gain_parts[0],
        triple_gradient,
        mixing_gradient,
        gain_parts[1],
        lifting_gradient,
        down_gradient,
    )


def solution(mesh):
    in_specs = (
        P("fsdp", "ctx", None),
        P("fsdp", "ctx", None),
        P("fsdp"),
        P("fsdp"),
        P("fsdp", None, "tp"),
        P("tp", "fsdp"),
        P("fsdp"),
        P("fsdp", None, "tp"),
        P("tp", "fsdp"),
    )
    out_specs = (
        P("fsdp", "ctx", None),
        P("fsdp", "ctx", None),
        P("fsdp"),
        P("fsdp", None, "tp"),
        P("tp", "fsdp"),
        P("fsdp"),
        P("fsdp", None, "tp"),
        P("tp", "fsdp"),
    )
    return jax.shard_map(
        functools.partial(on_device, sizes=dict(mesh.shape)),
        mesh=mesh,
        in_specs=in_specs,
        out_specs=out_specs,
        check_vma=False,
    )
```

```python
import functools

import jax
import jax.numpy as jnp
from jax import lax
from jax.experimental import pallas as pl
from jax.experimental.pallas import tpu as pltpu
from jax.sharding import PartitionSpec as P

H = 16
NORM_EPS = 1e-05
ROPE_BASE = 160000.0
MASKED = -1e30
LOG2E = 1.4426950408889634
BF = jnp.bfloat16
F32 = jnp.float32
FLOPS_PER_US = 1153e6
SCALE = 1.102
WEIGHTS = {"attention_grad": 1.116, "feed_grad1": 12.75, "halve": 6.466, "mix": 1.08, "norm_first_back": 0.2153, "pieces": 1.533, "project_back": 4.301, "sum_ctx": 4.169}
ORDER = (
    "SB0 EX PC0 SB1",
    "FG1 FG2 PC1 AB0",
    "I1 AB1 BR I2",
    "PB0 O1 PS0 PB1",
    "FB0 OT AT I3",
    "PS1 O2 I4 FB1",
    "A1 O3 JG A2",
    "OO O4 A3 A4",
    "OJ",
)
CORE, ROW = 1, 2


def nn(a, b):
    return lax.dot_general(a, b, (((1,), (0,)), ((), ())), preferred_element_type=F32)


def nt(a, b):
    return lax.dot_general(a, b, (((1,), (1,)), ((), ())), preferred_element_type=F32)


def tn(a, b):
    return lax.dot_general(a, b, (((0,), (0,)), ((), ())), preferred_element_type=F32)


def swap(array, axis, size, step):
    return lax.ppermute(array, axis, [(i, i ^ step) for i in range(size)])


def part(start, size):
    return pl.ds(pl.multiple_of(start * size, size), size)


def piece(refs, z, m):
    return refs[m] if len(refs) == 4 else refs[0].at[z ^ m]


class Part:
    def __init__(self, array, index):
        self.array, self.index = array, index


class Sequence:
    def __init__(self):
        self.last = None

    def __call__(self, body, scalars, arrays, outs, scratch=(), us=1, name=None, wait=(), mib=16):
        operands = [a.array if isinstance(a, Part) else a for a in arrays]
        specs = [pl.BlockSpec(memory_space=pltpu.VMEM)] * len(arrays)
        after = list(wait) + ([] if self.last is None else [self.last])
        first = len(scalars) + len(arrays)

        def run(*refs):
            taken = refs[len(scalars) : first]
            taken = [
                r.at[a.index] if isinstance(a, Part) else r
                for r, a in zip(taken, arrays, strict=True)
            ]
            body(*refs[: len(scalars)], *taken, *refs[first + len(after) :])

        results = pl.pallas_call(
            run,
            out_shape=[jax.ShapeDtypeStruct(s, t) for s, t in outs],
            in_specs=[pl.BlockSpec(memory_space=pltpu.SMEM)] * len(scalars)
            + specs
            + [pl.BlockSpec(memory_space=pl.ANY)] * len(after),
            out_specs=[pl.BlockSpec(memory_space=pltpu.VMEM)] * len(outs),
            scratch_shapes=list(scratch),
            compiler_params=pltpu.CompilerParams(vmem_limit_bytes=mib << 20),
            cost_estimate=pl.CostEstimate(
                flops=int(WEIGHTS.get(name, us) * SCALE * FLOPS_PER_US), bytes_accessed=0, transcendentals=0
            ),
            name=name,
        )(*scalars, *operands, *after)
        self.last = min(results, key=lambda r: r.size)
        return results


def whole_gain(gain, xi):
    own, other = gain[0:1, :].astype(F32), gain[1:2, :].astype(F32)
    low = jnp.where(xi == 0, own, other)
    high = jnp.where(xi == 0, other, own)
    return jnp.concatenate([low, high], axis=1)


def norm_body(place, x, gain, out):
    gain_row = whole_gain(gain, place[2])
    step = 256
    for s in range(x.shape[0]):

        def block(i, carry, s=s):
            at = part(i, step)
            v = x[s, at, :].astype(F32)
            center = v - jnp.mean(v, axis=-1, keepdims=True)
            spread = jnp.mean(center * center, axis=-1, keepdims=True)
            out[s, at, :] = (center * lax.rsqrt(spread + NORM_EPS) * gain_row).astype(BF)
            return carry

        lax.fori_loop(0, x.shape[1] // step, block, 0)


def project_body(size, kinds, place, *refs):
    normed, cosine, sine = refs[0:3]
    weights = refs[3 : 3 + 2 * len(kinds)]
    outs, heads = refs[3 + 2 * len(kinds) : -1], refs[-1]
    count = len(outs)
    half = weights[0].shape[0]
    z, xi = place[0], place[2]
    blocks = normed.shape[0] if len(normed.shape) == 3 else 1
    span = normed.shape[-2]
    for s in range(blocks):
        rows = slice(s * span, (s + 1) * span)
        source = normed.at[s] if len(normed.shape) == 3 else normed
        n_own = source[:, part(xi, half)]
        n_other = source[:, part(1 - xi, half)]
        for i, rotated in enumerate(kinds):
            acc = nt(weights[2 * i][...].T, n_own) + nt(weights[2 * i + 1][...].T, n_other)
            for h in range(count):
                u = acc[h * size : (h + 1) * size]
                if rotated:
                    u1, u2 = u[: size // 2], u[size // 2 :]
                    co, si = cosine[...], sine[...]
                    u = jnp.concatenate([u1 * co - u2 * si, u2 * co + u1 * si], axis=0)
                heads[h, i * size : (i + 1) * size, rows] = u.astype(BF)
    for m in range(count):
        outs[m][...] = heads[z ^ m]


def attend_body(s, span, place, lengths, *refs):
    k, qv = refs[0:4], refs[4:8]
    *o, o_full, lse, keys, values, top, total = refs[8:]
    z = place[0]
    size = k[0].shape[0]
    cols = slice(s * span, (s + 1) * span)
    values[:, size:, :] = jnp.ones((4, values.shape[1] - size, span), BF)
    for m in range(4):
        keys[z ^ m] = k[m][:, cols].T
        values[z ^ m, :size, :] = qv[m][size:, :]
    top[...] = jnp.full_like(top, MASKED)
    total[...] = jnp.zeros_like(total)
    length = lengths[s]
    full = length // span
    rest = length - full * span
    unit = size**-0.5 * LOG2E

    def step(j, limit):
        key, value = keys[j], values[j]
        for m in range(4):
            raw = nn(key, qv[m][:size, :])
            if limit is not None:
                raw = jnp.where(lax.broadcasted_iota(jnp.int32, raw.shape, 0) < limit, raw, MASKED)
            before = top[m : m + 1, :]
            peak = jnp.maximum(before, jnp.max(raw, axis=0, keepdims=True))
            p = jnp.exp2((raw - peak) * unit)
            top[m : m + 1, :] = peak
            total[m] = total[m] * jnp.exp2((before - peak) * unit) + nn(value, p.astype(BF))

    def whole(j, carry):
        step(j, None)
        return carry

    lax.fori_loop(0, full, whole, 0)

    @pl.when(rest > 0)
    def _():
        step(full, rest)

    for m in range(4):
        normaliser = total[m, size : size + 1, :]
        result = total[m, :size, :] / normaliser
        o_full[m] = result
        piece(o, z, m)[...] = result.astype(BF)
        lse[m : m + 1, :] = top[m : m + 1, :] * unit + jnp.log(normaliser) * LOG2E


def attend_back_body(s, span, place, lengths, *refs):
    k, qv = refs[0:4], refs[4:8]
    keys, keys_t, values, d_query, d_key, d_value, queries, grads, delta = refs[-9:]
    count = (len(refs) - 21) // 2
    do, out = refs[8 : 8 + count], refs[12 + count : -9]
    o_full, lse, cosine, sine = refs[8 + count : 12 + count]
    z = place[0]
    size = k[0].shape[0]
    cols = slice(s * span, (s + 1) * span)
    for m in range(4):
        keys[z ^ m] = k[m][:, cols].T
        keys_t[z ^ m] = k[m][:, cols]
        values[z ^ m] = qv[m][size:, :].T
        queries[m] = qv[m][:size, :].T
        grads[m] = piece(do, z, m)[...].T
        delta[m : m + 1, :] = jnp.sum(piece(do, z, m)[...].astype(F32) * o_full[m], axis=0, keepdims=True)
    d_query[...] = jnp.zeros_like(d_query)
    d_key[...] = jnp.zeros_like(d_key)
    d_value[...] = jnp.zeros_like(d_value)
    length = lengths[s]
    full = length // span
    rest = length - full * span
    factor = size**-0.5

    def step(j, limit):
        key, key_t, value = keys[j], keys_t[j], values[j]
        for m in range(4):
            raw = nn(key, qv[m][:size, :])
            if limit is not None:
                raw = jnp.where(lax.broadcasted_iota(jnp.int32, raw.shape, 0) < limit, raw, MASKED)
            p = jnp.exp2(raw * (factor * LOG2E) - lse[m : m + 1, :])
            dp = nn(value, piece(do, z, m)[...])
            ds = (p * (dp - delta[m : m + 1, :])).astype(BF)
            d_value[j] += nn(p.astype(BF), grads[m])
            d_key[j] += nn(ds, queries[m])
            d_query[m] += nn(key_t, ds)

    def whole(j, carry):
        step(j, None)
        return carry

    lax.fori_loop(0, full, whole, 0)

    @pl.when(rest > 0)
    def _():
        step(full, rest)

    def back(w, j):
        at = part(j, span)
        co, si = cosine[:, at], sine[:, at]
        w1, w2 = w[: size // 2] * factor, w[size // 2 :] * factor
        return jnp.concatenate([w1 * co + w2 * si, w2 * co - w1 * si], axis=0).astype(BF)

    for m in range(4):
        j = z ^ m
        target = piece(out, z, m)
        target[0:size, :] = back(d_query[m], j)
        target[size : 2 * size, :] = back(d_key[j].T, j)
        target[2 * size :, :] = d_value[j].T.astype(BF)


def heads_body(place, *refs):
    *o, mixed = refs
    size = mixed.shape[0] // 4
    for m in range(4):
        mixed[part(place[0] ^ m, size), :] = piece(o, place[0], m)[...]


def mix_body(place, mixed, *refs):
    *weights, out = refs
    c, xi = place[1], place[2]
    width, half = weights[0].shape
    rows = out.shape[0]
    left = [mixed[part(at, width), part(c, rows)].T for at in (c, 1 - c)]
    for side, hi in ((0, xi), (1, 1 - xi)):
        total = nn(left[0], weights[side][...]) + nn(left[1], weights[2 + side][...])
        out[:, part(hi, half)] = total.astype(BF)


def add_body(a, b, out):
    out[...] = (a[...].astype(F32) + b[...].astype(F32)).astype(out.dtype)


def feed_body(place, mine, theirs, x, gain, cot, *refs):
    weights = refs[0:4]
    middle, out, out_grad, *packs = refs[4:]
    c, xi = place[1], place[2]
    rows, width = middle.shape
    half = width // 2
    units = weights[0].shape[0] // 3
    lanes = (packs[0].shape[1] - width) // 3
    token_rows = part(c, rows)
    v = x[token_rows, :].astype(F32) + (mine[...].astype(F32) + theirs[...].astype(F32))
    middle[...] = v
    center = v - jnp.mean(v, axis=-1, keepdims=True)
    spread = jnp.mean(center * center, axis=-1, keepdims=True)
    n = (center * lax.rsqrt(spread + NORM_EPS) * whole_gain(gain, place[2])).astype(BF)
    columns = (part(xi, half), part(1 - xi, half))
    packs[0][:, :width] = n
    packs[1][:, :width] = n
    totals, totals_grad = [None, None], [None, None]
    for i, pack in enumerate(packs):
        sides = weights[2 * i : 2 * i + 2]

        def over(left, rows_of, sides=sides):
            return sum(nt(left(cols), w[rows_of, :]) for w, cols in zip(sides, columns))

        inner, gate, down = (slice(k * units, (k + 1) * units) for k in range(3))
        a = over(lambda cols, pack=pack: pack[:, cols], inner)
        b = over(lambda cols, pack=pack: pack[:, cols], gate)
        dh = over(lambda cols: cot[token_rows, cols], down)
        cdf = 0.5 * (1.0 + lax.erf(a * (0.5**0.5)))
        act = a * cdf
        slope = cdf + a * jnp.exp(-0.5 * a * a) * (0.5 * 2.0**0.5 / jnp.pi**0.5)
        h = (act * b).astype(BF)
        da = (dh * b * slope).astype(BF)
        db = (dh * act).astype(BF)
        for k, value in enumerate((h, da, db)):
            pack[:, width + k * lanes : width + k * lanes + units] = value
        for side, w in enumerate(sides):
            term = nn(da, w[inner, :]) + nn(db, w[gate, :])
            totals_grad[side] = term if i == 0 else totals_grad[side] + term
            term = nn(h, w[down, :])
            totals[side] = term if i == 0 else totals[side] + term
    for side, cols in enumerate(columns):
        out_grad[:, cols] = totals_grad[side].astype(BF)
        out[:, cols] = totals[side].astype(BF)


def feed_grad_body(units, kinds, place, *refs):
    *packs, cot, keep, send = refs
    c, xi = place[1], place[2]
    half = keep.shape[1]
    rows, lanes = packs[0].shape
    lanes = (lanes - 2 * half) // 3
    for target, hi in ((send, 1 - xi), (keep, xi)):
        for row, kind in enumerate(kinds):
            total = None
            for i, pack in enumerate(packs):
                start = 2 * half + kind * lanes
                if kind == 0:
                    right = cot[i // 2, part(c if i % 2 == 0 else 1 - c, rows), part(hi, half)]
                else:
                    right = pack[:, part(hi, half)]
                term = tn(pack[:, start : start + units], right)
                total = term if total is None else total + term
            target[row * units : (row + 1) * units, :] = total.astype(target.dtype)


def attention_grad_body(place, *refs):
    stacks, (normed,), gains, mixed, branches = refs[0:2], refs[2:3], refs[3:7], refs[7:9], refs[9:13]
    keep, send = refs[13:]
    c, xi = place[1], place[2]
    half = keep.shape[1]
    rows = stacks[0].shape[0]
    width = rows // 3
    under = keep.shape[0] - rows - width
    tokens = branches[0].shape[0]
    for target, hi in ((send, 1 - xi), (keep, xi)):
        cols = part(hi, half)
        total = nn(stacks[0][...], normed[0, :, cols]) + nn(stacks[1][...], normed[1, :, cols])
        target[0:rows, :] = total.astype(target.dtype)
        first = gains[0][:, cols] + gains[1][:, cols]
        second = 0.5 * (gains[2][:, cols] + gains[3][:, cols])
        which = lax.broadcasted_iota(jnp.int32, (under, half), 0)
        both = jnp.where(which == 0, first, jnp.where(which == 1, second, 0.0))
        target[rows : rows + under, :] = both.astype(target.dtype)
        total = None
        for s in range(2):
            for side, at in ((0, c), (1, 1 - c)):
                left = mixed[s][part(c, width), part(at, tokens)]
                term = nn(left, branches[2 * s + side][:, cols])
                total = term if total is None else total + term
        target[rows + under :, :] = total.astype(target.dtype)


def halve_body(which, place, a, b, keep, send):
    columns = keep.shape[1]
    for target, at in ((send, 1 - place[which]), (keep, place[which])):
        cols = part(at, columns)
        total = a[:, cols].astype(F32) + b[:, cols].astype(F32)
        target[...] = total.astype(target.dtype)


def unite_body(which, place, mine, theirs, out):
    columns = mine.shape[1]
    out[:, part(place[which], columns)] = mine[...].astype(out.dtype)
    out[:, part(1 - place[which], columns)] = theirs[...].astype(out.dtype)


def feed_end_body(which, place, mine0, theirs0, mine1, theirs1, lifting, down):
    columns = mine0.shape[1]
    units = down.shape[0]
    for first, second, at in ((mine0, mine1, place[which]), (theirs0, theirs1, 1 - place[which])):
        cols = part(at, columns)
        lifting[0, :, cols] = first[...].astype(F32)
        lifting[1, :, cols] = second[0:units, :].astype(F32)
        down[:, cols] = second[units:, :].astype(F32)


def attention_end_body(which, place, mine, theirs, triple, mixing, gains):
    columns = mine.shape[1]
    width = triple.shape[2]
    for part_of, at in ((mine, place[which]), (theirs, 1 - place[which])):
        cols = part(at, columns)
        for kind in range(3):
            value = part_of[kind * width : (kind + 1) * width, :]
            triple[kind, cols, :] = value.T.astype(F32)
        gains[:, cols] = part_of[3 * width : 3 * width + 16, :].astype(F32)[0:2]
        mixing[:, cols] = part_of[part_of.shape[0] - width :, :].astype(F32)


def norm_back(v, gain, grad):
    center = v - jnp.mean(v, axis=-1, keepdims=True)
    spread = jnp.mean(center * center, axis=-1, keepdims=True)
    r = lax.rsqrt(spread + NORM_EPS)
    xhat = center * r
    eg = grad * gain
    mean_eg = jnp.mean(eg, axis=-1, keepdims=True)
    mean_egx = jnp.mean(eg * xhat, axis=-1, keepdims=True)
    back = r * (eg - mean_eg - xhat * mean_egx)
    return back, jnp.sum(grad * xhat, axis=0, keepdims=True)


def second_back_body(place, mine, theirs, middle, cot, gain, *refs):
    *weights, middle_grad, branch, gain_grad, product = refs
    c, xi = place[1], place[2]
    rows = middle.shape[0]
    heads_width, half = weights[0].shape
    grad = mine[...].astype(F32) + theirs[...].astype(F32)
    back, total = norm_back(middle[...], whole_gain(gain, xi), grad)
    result = cot[part(c, rows), :].astype(F32) + back
    middle_grad[...] = result
    branch[...] = result.astype(BF)
    gain_grad[...] = total
    left, right = branch[:, part(xi, half)], branch[:, part(1 - xi, half)]
    for i, at in ((0, c), (1, 1 - c)):
        term = nt(weights[2 * i][...], left) + nt(weights[2 * i + 1][...], right)
        product[part(at, heads_width), :] = term.astype(BF)


def pieces_body(place, product, *outs):
    z, c = place[0], place[1]
    rows, columns = product.shape
    size = rows // 16
    for m in range(4):
        for k in range(2):
            rows_here = part(8 * k + 4 * c + (z ^ m), size)
            piece(outs, z, m)[:, k * columns : (k + 1) * columns] = product[rows_here, :]


def first_back_body(place, mine, theirs, x, middle_grad, gain, out):
    rows = middle_grad.shape[0]
    grad = mine[...].astype(F32) + theirs[...].astype(F32)
    back, _ = norm_back(x[part(place[1], rows), :].astype(F32), whole_gain(gain, place[2]), grad)
    out[...] = (middle_grad[...] + back).astype(BF)


def output_body(place, m0, m1, f0, f1, theirs, out):
    for s, (m, f) in enumerate(((m0, f0), (m1, f1))):
        out[s] = (m[...] + (f[...].astype(F32) + theirs[s].astype(F32))).astype(BF)


def join_body(place, *refs):
    *parts, out = refs
    rows = parts[0].shape[0]
    for s in range(len(parts) // 2):
        out[s, part(place[1], rows), :] = parts[2 * s][...]
        out[s, part(1 - place[1], rows), :] = parts[2 * s + 1][...]


def join_stacked_body(place, own, other, out):
    rows = own.shape[1]
    out[:, part(place[1], rows), :] = own[...]
    out[:, part(1 - place[1], rows), :] = other[...]


def project_back_body(place, *refs):
    *d, x = refs[:-10]
    weights, (keep, send, stacked, gain_grad) = refs[-10:-4], refs[-4:]
    c, rows = place[1], keep.shape[0]
    z, xi = place[0], place[2]
    half, width = weights[0].shape
    size = d[0].shape[-2] // 3
    for m in range(4):
        here = piece(d, z, m)
        for kind in range(3):
            at = part(kind * (width // size) + (z ^ m), size)
            stacked[at, :] = here[kind * size : (kind + 1) * size, :]
    for target, at in ((send, 1 - c), (keep, c)):
        tokens = stacked[:, part(at, rows)].T
        v = x[part(at, rows), :].astype(F32)
        mean = jnp.mean(v, axis=-1, keepdims=True)
        center = v - mean
        r = lax.rsqrt(jnp.mean(center * center, axis=-1, keepdims=True) + NORM_EPS)
        for side, hi in ((0, xi), (1, 1 - xi)):
            total = None
            for kind in range(3):
                term = nt(
                    tokens[:, kind * width : (kind + 1) * width], weights[2 * kind + side][...]
                )
                total = term if total is None else total + term
            cols = part(hi, half)
            target[:, cols] = total.astype(target.dtype)
            xhat = (x[part(at, rows), cols].astype(F32) - mean) * r
            sums = jnp.sum(total * xhat, axis=0, keepdims=True)
            if target is send:
                gain_grad[:, cols] = sums
            else:
                gain_grad[:, cols] += sums


def on_device(
    inputs,
    cotangent,
    lengths,
    attention_gain,
    triple_weight,
    mixing_weight,
    feedforward_gain,
    lifting_weight,
    down_weight,
    sizes,
):
    run = Sequence()
    pairs = sizes["fsdp"] == 2
    sequences, span, width = inputs.shape
    half = width // 2
    heads_width = triple_weight.shape[2]
    size = width // H
    heads = heads_width // size
    units = down_weight.shape[0]
    z = lax.axis_index("ctx")
    core = lax.axis_index("tp") % 2
    xi = lax.axis_index("fsdp") if pairs else jnp.int32(0)
    place = jnp.stack([z, core, xi, z % 2, z // 2]).astype(jnp.int32)
    quarter = span // 2
    both = range(sequences)

    def gather(array, axis):
        if pairs:
            return array, swap(array, "fsdp", 2, 1)
        full = lax.all_gather(array, "fsdp", axis=axis, tiled=True)
        return lax.split(full, [full.shape[axis] // 2] * 2, axis=axis)

    def over_fsdp(keep, send):
        if pairs:
            return keep, swap(send, "fsdp", 2, 1)
        full = jnp.concatenate([keep.astype(BF), send], axis=1)
        keep = lax.psum_scatter(full, "fsdp", scatter_dimension=1, tiled=True)
        return keep, jnp.zeros_like(keep)

    def added(a, b, kind, name):
        return run(add_body, [], [a, b], [(b.shape, kind)], name=name)[0]

    cores = [[0, 1], [2, 3]]

    def both_cores(array):
        return lax.all_gather(array, "tp", axis_index_groups=cores, axis=0, tiled=True)

    def redistribute(pieces):
        moved = {m: swap(pieces[m], "ctx", 4, m) for m in (2, 3, 1)}
        return [pieces[0], moved[1], moved[2], moved[3]]

    low, high = 3, 4

    class Reduction:
        def __init__(self, keep, send):
            self.a, self.b = over_fsdp(keep, send)
            if not pairs:
                self.a = lax.psum(self.a, "ctx").astype(F32)

        def halve(self, which, step):
            if not pairs:
                return
            rows, columns = self.a.shape
            shape = (rows, columns // 2)
            self.a, send = run(
                functools.partial(halve_body, which),
                [place],
                [self.a, self.b],
                [(shape, F32), (shape, BF)],
                us=1,
                name="halve",
            )
            self.b = swap(send, "ctx", 4, step)

        def unite(self, which, kind):
            if not pairs:
                return
            rows, columns = self.b.shape
            shape = (rows, columns * 2)
            (self.a,) = run(
                functools.partial(unite_body, which),
                [place],
                [self.a, self.b],
                [(shape, kind)],
                us=0.7,
                name="unite",
            )

        def first(self):
            self.halve(low, 1)

        def second(self):
            self.halve(high, 2)

        def third(self):
            if not pairs:
                return
            (self.a,) = run(
                add_body, [], [self.a, self.b], [(self.b.shape, BF)], us=0.4, name="sum_ctx"
            )
            self.b = swap(self.a, "ctx", 4, 2)

        def fourth(self):
            if not pairs:
                return
            self.unite(high, BF)
            self.b = swap(self.a, "ctx", 4, 1)

    key_w = gather(triple_weight[:, 1], 0)
    gains_own, gains_other = gather(jnp.stack([attention_gain, feedforward_gain]), 1)
    first_gain = jnp.stack([gains_own[0], gains_other[0]])
    second_gain = jnp.stack([gains_own[1], gains_other[1]])

    full_length = span * sizes["ctx"]
    frequency = ROPE_BASE ** (-2.0 * jnp.arange(size // 2, dtype=F32) / size)
    angles = frequency[:, None] * jnp.arange(full_length, dtype=jnp.int32).astype(F32)[None, :]
    cosine, sine = jnp.cos(angles), jnp.sin(angles)
    cosine_here = lax.dynamic_slice_in_dim(cosine, z * span, span, 1)
    sine_here = lax.dynamic_slice_in_dim(sine, z * span, span, 1)

    (normed_first,) = run(
        norm_body, [place], [inputs, first_gain], [(inputs.shape, BF)], name="norm_first"
    )

    def later(array):
        return lax.optimization_barrier((array, run.last))[0]

    query_w = gather(later(triple_weight[:, 0]), 0)
    value_w = gather(later(triple_weight[:, 2]), 0)

    def project(normed, kinds, weights, columns, wait=()):
        return redistribute(
            run(
                functools.partial(project_body, size, kinds),
                [place],
                [normed, cosine_here, sine_here, *weights],
                [((len(kinds) * size, columns), BF)] * heads,
                scratch=[pltpu.VMEM((heads, len(kinds) * size, columns), BF)],
                us=1.3,
                wait=wait,
                name="project",
            )
        )

    keys = project(normed_first, (True,), key_w, sequences * span)
    feed_own = jnp.concatenate(
        [lifting_weight[:, 0].T, lifting_weight[:, 1].T, down_weight], axis=0
    )
    first, second = Part(normed_first, 0), Part(normed_first, 1)
    mixing_w = gather(later(mixing_weight), 1)
    rest = [project(first, (True, False), (*query_w, *value_w), span, keys[1:3])]
    feed_w = gather(later(feed_own), 1)
    waits = [keys[3], rest[0][1], mixing_w[1]]
    rest.append(project(second, (True, False), (*query_w, *value_w), span, waits))

    attended = []

    def attend(s, wait):
        *o, o_full, lse = run(
            functools.partial(attend_body, s, span),
            [place, lengths],
            [*keys, *rest[s]],
            [*[((size, span), BF)] * 4, ((4, size, span), F32), ((4, span), F32)],
            scratch=[
                pltpu.VMEM((4, span, size), BF),
                pltpu.VMEM((4, size + 16, span), BF),
                pltpu.VMEM((4, span), F32),
                pltpu.VMEM((4, size + 16, span), F32),
            ],
            us=10,
            wait=wait,
            name="attend",
        )
        attended.append((redistribute(o), o_full, lse))

    attend(0, [])
    attend(1, [])

    mixtures, sums, mixing_all = [], [], list(mixing_w)

    def mix(s, wait):
        (mixed,) = run(
            heads_body,
            [place],
            attended[s][0],
            [((heads_width, span), BF)],
            us=0.6,
            wait=wait,
            name="heads",
        )
        if s == 0:
            mixing_all.extend(swap(later(w), "tp", 4, CORE) for w in mixing_w)
        mixed = both_cores(mixed)
        mixtures.append(mixed)
        (mine,) = run(
            mix_body, [place], [mixed, *mixing_all], [((quarter, width), BF)], us=1, name="mix"
        )
        sums.append((mine, swap(mine, "tp", 4, ROW)))

    mix(0, [])
    feed_theirs = [swap(later(w), "tp", 4, CORE) for w in feed_w]
    mix(1, [])

    feeds, grads, packs = [], [], []
    lanes = -(-units // 128) * 128
    for s in both:
        feed = run(
            feed_body,
            [place],
            [*sums[s], Part(inputs, s), second_gain, Part(cotangent, s), *feed_w, *feed_theirs],
            [
                ((quarter, width), F32),
                ((quarter, width), BF),
                ((quarter, width), BF),
                ((quarter, width + 3 * lanes), BF),
                ((quarter, width + 3 * lanes), BF),
            ],
            us=6.6,
            name="feed",
        )
        feeds.append(feed)
        grads.append((feed[2], swap(feed[2], "tp", 4, ROW)))
        packs.append((feed[3], feed[4]))
    rows = 3 * heads_width
    branches, middle_grads, gain_second, mixture_grads = {}, {}, {}, {}
    products, exchanged, reductions, d, partials = {}, [], {}, {}, {}
    stacks, gain_first, back_sums, inputs_own, made = {}, {}, {}, {}, {}

    def second_back(s):
        middle_grads[s], branches[s], gain_second[s], products[s] = run(
            second_back_body,
            [place],
            [*grads[s], feeds[s][0], Part(cotangent, s), second_gain, *mixing_all],
            [
                ((quarter, width), F32),
                ((quarter, width), BF),
                ((1, width), F32),
                ((2 * heads_width, quarter), BF),
            ],
            us=2,
            name="norm_second_back",
        )

    def pieces(s):
        cut = run(
            pieces_body,
            [place],
            [both_cores(products[s])],
            [((size, span), BF)] * 4,
            us=0.6,
            name="pieces",
        )
        mixture_grads[s] = redistribute(cut)

    def exchange_packs():
        for mine, theirs in packs:
            exchanged.extend([mine, swap(later(theirs), "tp", 4, CORE)])

    def feed_grad(key, kinds):
        count = len(kinds) * units
        reductions[key] = Reduction(
            *run(
                functools.partial(feed_grad_body, units, kinds),
                [place],
                [*exchanged, cotangent],
                [((count, half), F32), ((count, half), BF)],
                us=1.7 * len(kinds),
                name="feed_grad" + str(len(kinds)),
            )
        )

    def attend_back(s):
        _, o_full, lse = attended[s]
        d[s] = redistribute(
            run(
                functools.partial(attend_back_body, s, span),
                [place, lengths],
                [*keys, *rest[s], *mixture_grads[s], o_full, lse, cosine, sine],
                [((3 * size, span), BF)] * 4,
                scratch=[
                    pltpu.VMEM((4, span, size), BF),
                    pltpu.VMEM((4, size, span), BF),
                    pltpu.VMEM((4, span, size), BF),
                    pltpu.VMEM((4, size, span), F32),
                    pltpu.VMEM((4, span, size), F32),
                    pltpu.VMEM((4, span, size), F32),
                    pltpu.VMEM((4, span, size), BF),
                    pltpu.VMEM((4, span, size), BF),
                    pltpu.VMEM((4, span), F32),
                ],
                us=13,
                name="attend_back",
            )
        )

    def project_back(s):
        keep, send, stacks[s], gain_first[s] = run(
            project_back_body,
            [place],
            [*d[s], Part(inputs, s), *query_w, *key_w, *value_w],
            [
                ((quarter, width), F32),
                ((quarter, width), BF),
                ((3 * heads_width, span), BF),
                ((1, width), F32),
            ],
            us=2.4,
            name="project_back",
        )
        partials[s] = (keep, swap(send, "tp", 4, CORE))

    def project_sum(s):
        (mine,) = run(
            add_body, [], partials[s], [((quarter, width), BF)], us=0.4, name="project_sum"
        )
        back_sums[s] = (mine, swap(mine, "tp", 4, ROW))

    def first_back(s):
        (own,) = run(
            first_back_body,
            [place],
            [*back_sums[s], Part(inputs, s), middle_grads[s], first_gain],
            [((quarter, width), BF)],
            us=1.3,
            name="norm_first_back",
        )
        inputs_own[s] = (own, swap(own, "tp", 4, CORE))

    def exchange_branches():
        made["branches"] = [
            b for s in both for b in (branches[s], swap(later(branches[s]), "tp", 4, CORE))
        ]

    def attention_grad():
        sums = [gain_first[0], gain_first[1], gain_second[0], gain_second[1]]
        reductions["A"] = Reduction(
            *run(
                attention_grad_body,
                [place],
                [stacks[0], stacks[1], normed_first, *sums, *mixtures, *made["branches"]],
                [
                    ((rows + 16 + heads_width, half), F32),
                    ((rows + 16 + heads_width, half), BF),
                ],
                us=4.5,
                name="attention_grad",
            )
        )

    def output_start():
        made["out"] = swap(later(jnp.stack([f[1] for f in feeds])), "tp", 4, ROW)

    def output_own():
        (own,) = run(
            output_body,
            [place],
            [*[f[0] for f in feeds], *[f[1] for f in feeds], made["out"]],
            [((sequences, quarter, width), BF)],
            name="output",
        )
        made["out"] = (own, swap(own, "tp", 4, CORE))

    def output_join():
        (made["output"],) = run(
            join_stacked_body, [place], made["out"], [(inputs.shape, BF)], name="output_join"
        )

    def gradient_join():
        (made["gradient"],) = run(
            join_body,
            [place],
            [*inputs_own[0], *inputs_own[1]],
            [(inputs.shape, BF)],
            name="gradient_join",
        )

    steps = {
        "EX": exchange_packs,
        "FG1": lambda: feed_grad("I", (1,)),
        "FG2": lambda: feed_grad("O", (2, 0)),
        "BR": exchange_branches,
        "AT": attention_grad,
        "OT": output_start,
        "OO": output_own,
        "OJ": output_join,
        "JG": gradient_join,
    }
    for s in both:
        steps["SB" + str(s)] = functools.partial(second_back, s)
        steps["PC" + str(s)] = functools.partial(pieces, s)
        steps["AB" + str(s)] = functools.partial(attend_back, s)
        steps["PB" + str(s)] = functools.partial(project_back, s)
        steps["PS" + str(s)] = functools.partial(project_sum, s)
        steps["FB" + str(s)] = functools.partial(first_back, s)
    for line in ORDER:
        for step in line.split():
            if step in steps:
                steps[step]()
            else:
                stage = ("first", "second", "third", "fourth")[int(step[1]) - 1]
                getattr(reductions[step[0]], stage)()
    inner_grad, other_grad, attention_grad = (reductions[k] for k in "IOA")
    output, input_gradient = made["output"], made["gradient"]
    if pairs:
        lifting_gradient, down_gradient = run(
            functools.partial(feed_end_body, low),
            [place],
            [inner_grad.a, inner_grad.b, other_grad.a, other_grad.b],
            [((2, units, half), F32), ((units, half), F32)],
            us=2.5,
            name="feed_end",
        )
        triple_gradient, mixing_gradient, gain_parts = run(
            functools.partial(attention_end_body, low),
            [place],
            [attention_grad.a, attention_grad.b],
            [((3, half, heads_width), F32), ((heads_width, half), F32), ((2, half), F32)],
            us=2,
            name="attention_end",
        )
    else:
        lifting_gradient = jnp.stack([inner_grad.a, other_grad.a[:units]])
        down_gradient = other_grad.a[units:]
        total = attention_grad.a
        gain_parts = total[rows : rows + 2]
        triple_gradient = total[:rows].reshape(3, heads_width, -1).transpose(0, 2, 1)
        mixing_gradient = total[rows + 16 :]
    gain_parts = jnp.sum(lax.all_gather(gain_parts, "tp"), axis=0)
    lifting_gradient = lifting_gradient.transpose(2, 0, 1)
    triple_gradient = triple_gradient.transpose(1, 0, 2)

    return (
        output,
        input_gradient,
        gain_parts[0],
        triple_gradient,
        mixing_gradient,
        gain_parts[1],
        lifting_gradient,
        down_gradient,
    )


def solution(mesh):
    in_specs = (
        P("fsdp", "ctx", None),
        P("fsdp", "ctx", None),
        P("fsdp"),
        P("fsdp"),
        P("fsdp", None, "tp"),
        P("tp", "fsdp"),
        P("fsdp"),
        P("fsdp", None, "tp"),
        P("tp", "fsdp"),
    )
    out_specs = (
        P("fsdp", "ctx", None),
        P("fsdp", "ctx", None),
        P("fsdp"),
        P("fsdp", None, "tp"),
        P("tp", "fsdp"),
        P("fsdp"),
        P("fsdp", None, "tp"),
        P("tp", "fsdp"),
    )
    return jax.shard_map(
        functools.partial(on_device, sizes=dict(mesh.shape)),
        mesh=mesh,
        in_specs=in_specs,
        out_specs=out_specs,
        check_vma=False,
    )
```

```python
import functools

import jax
import jax.numpy as jnp
from jax import lax
from jax.experimental import pallas as pl
from jax.experimental.pallas import tpu as pltpu
from jax.sharding import PartitionSpec as P

H = 16
NORM_EPS = 1e-05
ROPE_BASE = 160000.0
MASKED = -1e30
LOG2E = 1.4426950408889634
BF = jnp.bfloat16
F32 = jnp.float32
FLOPS_PER_US = 1153e6
SCALE = 0.764
WEIGHTS = {"attend_back": 25.94, "attention_grad": 16.5, "feed": 3.975, "feed_grad1": 2.168, "gradient_join": 4.874, "halve": 6.466, "mix": 2.703, "norm_first_back": 0.02256, "output_join": 0.2996, "pieces": 0.09989, "project_back": 4.301, "project_sum": 0.2843, "sum_ctx": 4.169}
WAIT_KEYS, WAIT_REST, WAIT_MIXING = (1,), (1,), True
FETCH = {"keys": "mixing", "first": "feed"}
ORDER = (
    "SB0 PC0 SB1 EX",
    "AB0 FG1 PC1 FG2",
    "I1 AB1 BR I2",
    "PB0 O1 PS0 PB1",
    "FB0 AT PS1 OT",
    "I3 O2 FB1 I4",
    "A1 O3 OO A2",
    "O4 JG A3 A4",
    "OJ",
)
CORE, ROW = 1, 2


def nn(a, b):
    return lax.dot_general(a, b, (((1,), (0,)), ((), ())), preferred_element_type=F32)


def nt(a, b):
    return lax.dot_general(a, b, (((1,), (1,)), ((), ())), preferred_element_type=F32)


def tn(a, b):
    return lax.dot_general(a, b, (((0,), (0,)), ((), ())), preferred_element_type=F32)


def swap(array, axis, size, step):
    return lax.ppermute(array, axis, [(i, i ^ step) for i in range(size)])


def part(start, size):
    return pl.ds(pl.multiple_of(start * size, size), size)


def piece(refs, z, m):
    return refs[m] if len(refs) == 4 else refs[0].at[z ^ m]


class Part:
    def __init__(self, array, index):
        self.array, self.index = array, index


class Sequence:
    def __init__(self):
        self.last = None

    def __call__(self, body, scalars, arrays, outs, scratch=(), us=1, name=None, wait=(), mib=16):
        operands = [a.array if isinstance(a, Part) else a for a in arrays]
        specs = [pl.BlockSpec(memory_space=pltpu.VMEM)] * len(arrays)
        after = list(wait) + ([] if self.last is None else [self.last])
        first = len(scalars) + len(arrays)

        def run(*refs):
            taken = refs[len(scalars) : first]
            taken = [
                r.at[a.index] if isinstance(a, Part) else r
                for r, a in zip(taken, arrays, strict=True)
            ]
            body(*refs[: len(scalars)], *taken, *refs[first + len(after) :])

        results = pl.pallas_call(
            run,
            out_shape=[jax.ShapeDtypeStruct(s, t) for s, t in outs],
            in_specs=[pl.BlockSpec(memory_space=pltpu.SMEM)] * len(scalars)
            + specs
            + [pl.BlockSpec(memory_space=pl.ANY)] * len(after),
            out_specs=[pl.BlockSpec(memory_space=pltpu.VMEM)] * len(outs),
            scratch_shapes=list(scratch),
            compiler_params=pltpu.CompilerParams(vmem_limit_bytes=mib << 20),
            cost_estimate=pl.CostEstimate(
                flops=int(WEIGHTS.get(name, us) * SCALE * FLOPS_PER_US), bytes_accessed=0, transcendentals=0
            ),
            name=name,
        )(*scalars, *operands, *after)
        self.last = min(results, key=lambda r: r.size)
        return results


def whole_gain(gain, xi):
    own, other = gain[0:1, :].astype(F32), gain[1:2, :].astype(F32)
    low = jnp.where(xi == 0, own, other)
    high = jnp.where(xi == 0, other, own)
    return jnp.concatenate([low, high], axis=1)


def norm_body(place, x, gain, out):
    gain_row = whole_gain(gain, place[2])
    step = 256
    for s in range(x.shape[0]):

        def block(i, carry, s=s):
            at = part(i, step)
            v = x[s, at, :].astype(F32)
            center = v - jnp.mean(v, axis=-1, keepdims=True)
            spread = jnp.mean(center * center, axis=-1, keepdims=True)
            out[s, at, :] = (center * lax.rsqrt(spread + NORM_EPS) * gain_row).astype(BF)
            return carry

        lax.fori_loop(0, x.shape[1] // step, block, 0)


def project_body(size, kinds, place, *refs):
    normed, cosine, sine = refs[0:3]
    weights = refs[3 : 3 + 2 * len(kinds)]
    outs, heads = refs[3 + 2 * len(kinds) : -1], refs[-1]
    count = len(outs)
    half = weights[0].shape[0]
    z, xi = place[0], place[2]
    blocks = normed.shape[0] if len(normed.shape) == 3 else 1
    span = normed.shape[-2]
    for s in range(blocks):
        rows = slice(s * span, (s + 1) * span)
        source = normed.at[s] if len(normed.shape) == 3 else normed
        n_own = source[:, part(xi, half)]
        n_other = source[:, part(1 - xi, half)]
        for i, rotated in enumerate(kinds):
            acc = nt(weights[2 * i][...].T, n_own) + nt(weights[2 * i + 1][...].T, n_other)
            for h in range(count):
                u = acc[h * size : (h + 1) * size]
                if rotated:
                    u1, u2 = u[: size // 2], u[size // 2 :]
                    co, si = cosine[...], sine[...]
                    u = jnp.concatenate([u1 * co - u2 * si, u2 * co + u1 * si], axis=0)
                heads[h, i * size : (i + 1) * size, rows] = u.astype(BF)
    for m in range(count):
        outs[m][...] = heads[z ^ m]


def attend_body(s, span, place, lengths, *refs):
    k, qv = refs[0:4], refs[4:8]
    *o, o_full, lse, keys, values, top, total = refs[8:]
    z = place[0]
    size = k[0].shape[0]
    cols = slice(s * span, (s + 1) * span)
    values[:, size:, :] = jnp.ones((4, values.shape[1] - size, span), BF)
    for m in range(4):
        keys[z ^ m] = k[m][:, cols].T
        values[z ^ m, :size, :] = qv[m][size:, :]
    top[...] = jnp.full_like(top, MASKED)
    total[...] = jnp.zeros_like(total)
    length = lengths[s]
    full = length // span
    rest = length - full * span
    unit = size**-0.5 * LOG2E

    def step(j, limit):
        key, value = keys[j], values[j]
        for m in range(4):
            raw = nn(key, qv[m][:size, :])
            if limit is not None:
                raw = jnp.where(lax.broadcasted_iota(jnp.int32, raw.shape, 0) < limit, raw, MASKED)
            before = top[m : m + 1, :]
            peak = jnp.maximum(before, jnp.max(raw, axis=0, keepdims=True))
            p = jnp.exp2((raw - peak) * unit)
            top[m : m + 1, :] = peak
            total[m] = total[m] * jnp.exp2((before - peak) * unit) + nn(value, p.astype(BF))

    def whole(j, carry):
        step(j, None)
        return carry

    lax.fori_loop(0, full, whole, 0)

    @pl.when(rest > 0)
    def _():
        step(full, rest)

    for m in range(4):
        normaliser = total[m, size : size + 1, :]
        result = total[m, :size, :] / normaliser
        o_full[m] = result
        piece(o, z, m)[...] = result.astype(BF)
        lse[m : m + 1, :] = top[m : m + 1, :] * unit + jnp.log(normaliser) * LOG2E


def attend_back_body(s, span, place, lengths, *refs):
    k, qv = refs[0:4], refs[4:8]
    keys, keys_t, values, d_query, d_key, d_value, queries, grads, delta = refs[-9:]
    count = (len(refs) - 21) // 2
    do, out = refs[8 : 8 + count], refs[12 + count : -9]
    o_full, lse, cosine, sine = refs[8 + count : 12 + count]
    z = place[0]
    size = k[0].shape[0]
    cols = slice(s * span, (s + 1) * span)
    for m in range(4):
        keys[z ^ m] = k[m][:, cols].T
        keys_t[z ^ m] = k[m][:, cols]
        values[z ^ m] = qv[m][size:, :].T
        queries[m] = qv[m][:size, :].T
        grads[m] = piece(do, z, m)[...].T
        delta[m : m + 1, :] = jnp.sum(piece(do, z, m)[...].astype(F32) * o_full[m], axis=0, keepdims=True)
    d_query[...] = jnp.zeros_like(d_query)
    d_key[...] = jnp.zeros_like(d_key)
    d_value[...] = jnp.zeros_like(d_value)
    length = lengths[s]
    full = length // span
    rest = length - full * span
    factor = size**-0.5

    def step(j, limit):
        key, key_t, value = keys[j], keys_t[j], values[j]
        for m in range(4):
            raw = nn(key, qv[m][:size, :])
            if limit is not None:
                raw = jnp.where(lax.broadcasted_iota(jnp.int32, raw.shape, 0) < limit, raw, MASKED)
            p = jnp.exp2(raw * (factor * LOG2E) - lse[m : m + 1, :])
            dp = nn(value, piece(do, z, m)[...])
            ds = (p * (dp - delta[m : m + 1, :])).astype(BF)
            d_value[j] += nn(p.astype(BF), grads[m])
            d_key[j] += nn(ds, queries[m])
            d_query[m] += nn(key_t, ds)

    def whole(j, carry):
        step(j, None)
        return carry

    lax.fori_loop(0, full, whole, 0)

    @pl.when(rest > 0)
    def _():
        step(full, rest)

    def back(w, j):
        at = part(j, span)
        co, si = cosine[:, at], sine[:, at]
        w1, w2 = w[: size // 2] * factor, w[size // 2 :] * factor
        return jnp.concatenate([w1 * co + w2 * si, w2 * co - w1 * si], axis=0).astype(BF)

    for m in range(4):
        j = z ^ m
        target = piece(out, z, m)
        target[0:size, :] = back(d_query[m], j)
        target[size : 2 * size, :] = back(d_key[j].T, j)
        target[2 * size :, :] = d_value[j].T.astype(BF)


def heads_body(place, *refs):
    *o, mixed = refs
    size = mixed.shape[0] // 4
    for m in range(4):
        mixed[part(place[0] ^ m, size), :] = piece(o, place[0], m)[...]


def mix_body(place, mixed, *refs):
    *weights, out = refs
    c, xi = place[1], place[2]
    width, half = weights[0].shape
    rows = out.shape[0]
    left = [mixed[part(at, width), part(c, rows)].T for at in (c, 1 - c)]
    for side, hi in ((0, xi), (1, 1 - xi)):
        total = nn(left[0], weights[side][...]) + nn(left[1], weights[2 + side][...])
        out[:, part(hi, half)] = total.astype(BF)


def add_body(a, b, out):
    out[...] = (a[...].astype(F32) + b[...].astype(F32)).astype(out.dtype)


def feed_body(place, mine, theirs, x, gain, cot, *refs):
    weights = refs[0:4]
    middle, out, out_grad, *packs = refs[4:]
    c, xi = place[1], place[2]
    rows, width = middle.shape
    half = width // 2
    units = weights[0].shape[0] // 3
    lanes = (packs[0].shape[1] - width) // 3
    token_rows = part(c, rows)
    v = x[token_rows, :].astype(F32) + (mine[...].astype(F32) + theirs[...].astype(F32))
    middle[...] = v
    center = v - jnp.mean(v, axis=-1, keepdims=True)
    spread = jnp.mean(center * center, axis=-1, keepdims=True)
    n = (center * lax.rsqrt(spread + NORM_EPS) * whole_gain(gain, place[2])).astype(BF)
    columns = (part(xi, half), part(1 - xi, half))
    packs[0][:, :width] = n
    packs[1][:, :width] = n
    totals, totals_grad = [None, None], [None, None]
    for i, pack in enumerate(packs):
        sides = weights[2 * i : 2 * i + 2]

        def over(left, rows_of, sides=sides):
            return sum(nt(left(cols), w[rows_of, :]) for w, cols in zip(sides, columns))

        inner, gate, down = (slice(k * units, (k + 1) * units) for k in range(3))
        a = over(lambda cols, pack=pack: pack[:, cols], inner)
        b = over(lambda cols, pack=pack: pack[:, cols], gate)
        dh = over(lambda cols: cot[token_rows, cols], down)
        cdf = 0.5 * (1.0 + lax.erf(a * (0.5**0.5)))
        act = a * cdf
        slope = cdf + a * jnp.exp(-0.5 * a * a) * (0.5 * 2.0**0.5 / jnp.pi**0.5)
        h = (act * b).astype(BF)
        da = (dh * b * slope).astype(BF)
        db = (dh * act).astype(BF)
        for k, value in enumerate((h, da, db)):
            pack[:, width + k * lanes : width + k * lanes + units] = value
        for side, w in enumerate(sides):
            term = nn(da, w[inner, :]) + nn(db, w[gate, :])
            totals_grad[side] = term if i == 0 else totals_grad[side] + term
            term = nn(h, w[down, :])
            totals[side] = term if i == 0 else totals[side] + term
    for side, cols in enumerate(columns):
        out_grad[:, cols] = totals_grad[side].astype(BF)
        out[:, cols] = totals[side].astype(BF)


def feed_grad_body(units, kinds, place, *refs):
    *packs, cot, keep, send = refs
    c, xi = place[1], place[2]
    half = keep.shape[1]
    rows, lanes = packs[0].shape
    lanes = (lanes - 2 * half) // 3
    for target, hi in ((send, 1 - xi), (keep, xi)):
        for row, kind in enumerate(kinds):
            total = None
            for i, pack in enumerate(packs):
                start = 2 * half + kind * lanes
                if kind == 0:
                    right = cot[i // 2, part(c if i % 2 == 0 else 1 - c, rows), part(hi, half)]
                else:
                    right = pack[:, part(hi, half)]
                term = tn(pack[:, start : start + units], right)
                total = term if total is None else total + term
            target[row * units : (row + 1) * units, :] = total.astype(target.dtype)


def attention_grad_body(place, *refs):
    stacks, (normed,), gains, mixed, branches = refs[0:2], refs[2:3], refs[3:7], refs[7:9], refs[9:13]
    keep, send = refs[13:]
    c, xi = place[1], place[2]
    half = keep.shape[1]
    rows = stacks[0].shape[0]
    width = rows // 3
    under = keep.shape[0] - rows - width
    tokens = branches[0].shape[0]
    for target, hi in ((send, 1 - xi), (keep, xi)):
        cols = part(hi, half)
        total = nn(stacks[0][...], normed[0, :, cols]) + nn(stacks[1][...], normed[1, :, cols])
        target[0:rows, :] = total.astype(target.dtype)
        first = gains[0][:, cols] + gains[1][:, cols]
        second = 0.5 * (gains[2][:, cols] + gains[3][:, cols])
        which = lax.broadcasted_iota(jnp.int32, (under, half), 0)
        both = jnp.where(which == 0, first, jnp.where(which == 1, second, 0.0))
        target[rows : rows + under, :] = both.astype(target.dtype)
        total = None
        for s in range(2):
            for side, at in ((0, c), (1, 1 - c)):
                left = mixed[s][part(c, width), part(at, tokens)]
                term = nn(left, branches[2 * s + side][:, cols])
                total = term if total is None else total + term
        target[rows + under :, :] = total.astype(target.dtype)


def halve_body(which, place, a, b, keep, send):
    columns = keep.shape[1]
    for target, at in ((send, 1 - place[which]), (keep, place[which])):
        cols = part(at, columns)
        total = a[:, cols].astype(F32) + b[:, cols].astype(F32)
        target[...] = total.astype(target.dtype)


def unite_body(which, place, mine, theirs, out):
    columns = mine.shape[1]
    out[:, part(place[which], columns)] = mine[...].astype(out.dtype)
    out[:, part(1 - place[which], columns)] = theirs[...].astype(out.dtype)


def feed_end_body(which, place, mine0, theirs0, mine1, theirs1, lifting, down):
    columns = mine0.shape[1]
    units = down.shape[0]
    for first, second, at in ((mine0, mine1, place[which]), (theirs0, theirs1, 1 - place[which])):
        cols = part(at, columns)
        lifting[0, :, cols] = first[...].astype(F32)
        lifting[1, :, cols] = second[0:units, :].astype(F32)
        down[:, cols] = second[units:, :].astype(F32)


def attention_end_body(which, place, mine, theirs, triple, mixing, gains):
    columns = mine.shape[1]
    width = triple.shape[2]
    for part_of, at in ((mine, place[which]), (theirs, 1 - place[which])):
        cols = part(at, columns)
        for kind in range(3):
            value = part_of[kind * width : (kind + 1) * width, :]
            triple[kind, cols, :] = value.T.astype(F32)
        gains[:, cols] = part_of[3 * width : 3 * width + 16, :].astype(F32)[0:2]
        mixing[:, cols] = part_of[part_of.shape[0] - width :, :].astype(F32)


def norm_back(v, gain, grad):
    center = v - jnp.mean(v, axis=-1, keepdims=True)
    spread = jnp.mean(center * center, axis=-1, keepdims=True)
    r = lax.rsqrt(spread + NORM_EPS)
    xhat = center * r
    eg = grad * gain
    mean_eg = jnp.mean(eg, axis=-1, keepdims=True)
    mean_egx = jnp.mean(eg * xhat, axis=-1, keepdims=True)
    back = r * (eg - mean_eg - xhat * mean_egx)
    return back, jnp.sum(grad * xhat, axis=0, keepdims=True)


def second_back_body(place, mine, theirs, middle, cot, gain, *refs):
    *weights, middle_grad, branch, gain_grad, product = refs
    c, xi = place[1], place[2]
    rows = middle.shape[0]
    heads_width, half = weights[0].shape
    grad = mine[...].astype(F32) + theirs[...].astype(F32)
    back, total = norm_back(middle[...], whole_gain(gain, xi), grad)
    result = cot[part(c, rows), :].astype(F32) + back
    middle_grad[...] = result
    branch[...] = result.astype(BF)
    gain_grad[...] = total
    left, right = branch[:, part(xi, half)], branch[:, part(1 - xi, half)]
    for i, at in ((0, c), (1, 1 - c)):
        term = nt(weights[2 * i][...], left) + nt(weights[2 * i + 1][...], right)
        product[part(at, heads_width), :] = term.astype(BF)


def pieces_body(place, product, *outs):
    z, c = place[0], place[1]
    rows, columns = product.shape
    size = rows // 16
    for m in range(4):
        for k in range(2):
            rows_here = part(8 * k + 4 * c + (z ^ m), size)
            piece(outs, z, m)[:, k * columns : (k + 1) * columns] = product[rows_here, :]


def first_back_body(place, mine, theirs, x, middle_grad, gain, out):
    rows = middle_grad.shape[0]
    grad = mine[...].astype(F32) + theirs[...].astype(F32)
    back, _ = norm_back(x[part(place[1], rows), :].astype(F32), whole_gain(gain, place[2]), grad)
    out[...] = (middle_grad[...] + back).astype(BF)


def output_body(place, m0, m1, f0, f1, theirs, out):
    for s, (m, f) in enumerate(((m0, f0), (m1, f1))):
        out[s] = (m[...] + (f[...].astype(F32) + theirs[s].astype(F32))).astype(BF)


def join_body(place, *refs):
    *parts, out = refs
    rows = parts[0].shape[0]
    for s in range(len(parts) // 2):
        out[s, part(place[1], rows), :] = parts[2 * s][...]
        out[s, part(1 - place[1], rows), :] = parts[2 * s + 1][...]


def join_stacked_body(place, own, other, out):
    rows = own.shape[1]
    out[:, part(place[1], rows), :] = own[...]
    out[:, part(1 - place[1], rows), :] = other[...]


def project_back_body(place, *refs):
    *d, x = refs[:-10]
    weights, (keep, send, stacked, gain_grad) = refs[-10:-4], refs[-4:]
    c, rows = place[1], keep.shape[0]
    z, xi = place[0], place[2]
    half, width = weights[0].shape
    size = d[0].shape[-2] // 3
    for m in range(4):
        here = piece(d, z, m)
        for kind in range(3):
            at = part(kind * (width // size) + (z ^ m), size)
            stacked[at, :] = here[kind * size : (kind + 1) * size, :]
    for target, at in ((send, 1 - c), (keep, c)):
        tokens = stacked[:, part(at, rows)].T
        v = x[part(at, rows), :].astype(F32)
        mean = jnp.mean(v, axis=-1, keepdims=True)
        center = v - mean
        r = lax.rsqrt(jnp.mean(center * center, axis=-1, keepdims=True) + NORM_EPS)
        for side, hi in ((0, xi), (1, 1 - xi)):
            total = None
            for kind in range(3):
                term = nt(
                    tokens[:, kind * width : (kind + 1) * width], weights[2 * kind + side][...]
                )
                total = term if total is None else total + term
            cols = part(hi, half)
            target[:, cols] = total.astype(target.dtype)
            xhat = (x[part(at, rows), cols].astype(F32) - mean) * r
            sums = jnp.sum(total * xhat, axis=0, keepdims=True)
            if target is send:
                gain_grad[:, cols] = sums
            else:
                gain_grad[:, cols] += sums


def on_device(
    inputs,
    cotangent,
    lengths,
    attention_gain,
    triple_weight,
    mixing_weight,
    feedforward_gain,
    lifting_weight,
    down_weight,
    sizes,
):
    run = Sequence()
    pairs = sizes["fsdp"] == 2
    sequences, span, width = inputs.shape
    half = width // 2
    heads_width = triple_weight.shape[2]
    size = width // H
    heads = heads_width // size
    units = down_weight.shape[0]
    z = lax.axis_index("ctx")
    core = lax.axis_index("tp") % 2
    xi = lax.axis_index("fsdp") if pairs else jnp.int32(0)
    place = jnp.stack([z, core, xi, z % 2, z // 2]).astype(jnp.int32)
    quarter = span // 2
    both = range(sequences)

    def gather(array, axis):
        if pairs:
            return array, swap(array, "fsdp", 2, 1)
        full = lax.all_gather(array, "fsdp", axis=axis, tiled=True)
        return lax.split(full, [full.shape[axis] // 2] * 2, axis=axis)

    def over_fsdp(keep, send):
        if pairs:
            return keep, swap(send, "fsdp", 2, 1)
        full = jnp.concatenate([keep.astype(BF), send], axis=1)
        keep = lax.psum_scatter(full, "fsdp", scatter_dimension=1, tiled=True)
        return keep, jnp.zeros_like(keep)

    def added(a, b, kind, name):
        return run(add_body, [], [a, b], [(b.shape, kind)], name=name)[0]

    cores = [[0, 1], [2, 3]]

    def both_cores(array):
        return lax.all_gather(array, "tp", axis_index_groups=cores, axis=0, tiled=True)

    def redistribute(pieces):
        moved = {m: swap(pieces[m], "ctx", 4, m) for m in (2, 3, 1)}
        return [pieces[0], moved[1], moved[2], moved[3]]

    low, high = 3, 4

    class Reduction:
        def __init__(self, keep, send):
            self.a, self.b = over_fsdp(keep, send)
            if not pairs:
                self.a = lax.psum(self.a, "ctx").astype(F32)

        def halve(self, which, step):
            if not pairs:
                return
            rows, columns = self.a.shape
            shape = (rows, columns // 2)
            self.a, send = run(
                functools.partial(halve_body, which),
                [place],
                [self.a, self.b],
                [(shape, F32), (shape, BF)],
                us=1,
                name="halve",
            )
            self.b = swap(send, "ctx", 4, step)

        def unite(self, which, kind):
            if not pairs:
                return
            rows, columns = self.b.shape
            shape = (rows, columns * 2)
            (self.a,) = run(
                functools.partial(unite_body, which),
                [place],
                [self.a, self.b],
                [(shape, kind)],
                us=0.7,
                name="unite",
            )

        def first(self):
            self.halve(low, 1)

        def second(self):
            self.halve(high, 2)

        def third(self):
            if not pairs:
                return
            (self.a,) = run(
                add_body, [], [self.a, self.b], [(self.b.shape, BF)], us=0.4, name="sum_ctx"
            )
            self.b = swap(self.a, "ctx", 4, 2)

        def fourth(self):
            if not pairs:
                return
            self.unite(high, BF)
            self.b = swap(self.a, "ctx", 4, 1)

    key_w = gather(triple_weight[:, 1], 0)
    gains_own, gains_other = gather(jnp.stack([attention_gain, feedforward_gain]), 1)
    first_gain = jnp.stack([gains_own[0], gains_other[0]])
    second_gain = jnp.stack([gains_own[1], gains_other[1]])

    full_length = span * sizes["ctx"]
    frequency = ROPE_BASE ** (-2.0 * jnp.arange(size // 2, dtype=F32) / size)
    angles = frequency[:, None] * jnp.arange(full_length, dtype=jnp.int32).astype(F32)[None, :]
    cosine, sine = jnp.cos(angles), jnp.sin(angles)
    cosine_here = lax.dynamic_slice_in_dim(cosine, z * span, span, 1)
    sine_here = lax.dynamic_slice_in_dim(sine, z * span, span, 1)

    (normed_first,) = run(
        norm_body, [place], [inputs, first_gain], [(inputs.shape, BF)], name="norm_first"
    )

    def later(array):
        return lax.optimization_barrier((array, run.last))[0]

    query_w = gather(later(triple_weight[:, 0]), 0)
    value_w = gather(later(triple_weight[:, 2]), 0)

    def project(normed, kinds, weights, columns, wait=()):
        return redistribute(
            run(
                functools.partial(project_body, size, kinds),
                [place],
                [normed, cosine_here, sine_here, *weights],
                [((len(kinds) * size, columns), BF)] * heads,
                scratch=[pltpu.VMEM((heads, len(kinds) * size, columns), BF)],
                us=1.3,
                wait=wait,
                name="project",
            )
        )

    keys = project(normed_first, (True,), key_w, sequences * span)
    first, second = Part(normed_first, 0), Part(normed_first, 1)
    feed_own = jnp.concatenate(
        [lifting_weight[:, 0].T, lifting_weight[:, 1].T, down_weight], axis=0
    )
    fetched = {}

    def fetch(point):
        for name in FETCH.get(point, "").split():
            source = {"mixing": mixing_weight, "feed": feed_own}[name]
            fetched[name] = gather(later(source), 1)

    fetch("keys")
    rest = [project(first, (True, False), (*query_w, *value_w), span, [keys[i] for i in WAIT_KEYS])]
    fetch("first")
    waits = [keys[i] for i in (1, 2, 3) if i not in WAIT_KEYS]
    waits += [rest[0][i] for i in WAIT_REST]
    waits += [fetched["mixing"][1]] if WAIT_MIXING and "mixing" in fetched else []
    rest.append(project(second, (True, False), (*query_w, *value_w), span, waits))
    fetch("second")

    attended = []

    def attend(s, wait):
        *o, o_full, lse = run(
            functools.partial(attend_body, s, span),
            [place, lengths],
            [*keys, *rest[s]],
            [*[((size, span), BF)] * 4, ((4, size, span), F32), ((4, span), F32)],
            scratch=[
                pltpu.VMEM((4, span, size), BF),
                pltpu.VMEM((4, size + 16, span), BF),
                pltpu.VMEM((4, span), F32),
                pltpu.VMEM((4, size + 16, span), F32),
            ],
            us=10,
            wait=wait,
            name="attend",
        )
        attended.append((redistribute(o), o_full, lse))

    attend(0, [])
    fetch("attend")
    mixing_w, feed_w = fetched["mixing"], fetched["feed"]
    attend(1, [])

    mixtures, sums, mixing_all = [], [], list(mixing_w)

    def mix(s, wait):
        (mixed,) = run(
            heads_body,
            [place],
            attended[s][0],
            [((heads_width, span), BF)],
            us=0.6,
            wait=wait,
            name="heads",
        )
        if s == 0:
            mixing_all.extend(swap(later(w), "tp", 4, CORE) for w in mixing_w)
        mixed = both_cores(mixed)
        mixtures.append(mixed)
        (mine,) = run(
            mix_body, [place], [mixed, *mixing_all], [((quarter, width), BF)], us=1, name="mix"
        )
        sums.append((mine, swap(mine, "tp", 4, ROW)))

    mix(0, [])
    feed_theirs = [swap(later(w), "tp", 4, CORE) for w in feed_w]
    mix(1, [])

    feeds, grads, packs = [], [], []
    lanes = -(-units // 128) * 128
    for s in both:
        feed = run(
            feed_body,
            [place],
            [*sums[s], Part(inputs, s), second_gain, Part(cotangent, s), *feed_w, *feed_theirs],
            [
                ((quarter, width), F32),
                ((quarter, width), BF),
                ((quarter, width), BF),
                ((quarter, width + 3 * lanes), BF),
                ((quarter, width + 3 * lanes), BF),
            ],
            us=6.6,
            name="feed",
        )
        feeds.append(feed)
        grads.append((feed[2], swap(feed[2], "tp", 4, ROW)))
        packs.append((feed[3], feed[4]))
    rows = 3 * heads_width
    branches, middle_grads, gain_second, mixture_grads = {}, {}, {}, {}
    products, exchanged, reductions, d, partials = {}, [], {}, {}, {}
    stacks, gain_first, back_sums, inputs_own, made = {}, {}, {}, {}, {}

    def second_back(s):
        middle_grads[s], branches[s], gain_second[s], products[s] = run(
            second_back_body,
            [place],
            [*grads[s], feeds[s][0], Part(cotangent, s), second_gain, *mixing_all],
            [
                ((quarter, width), F32),
                ((quarter, width), BF),
                ((1, width), F32),
                ((2 * heads_width, quarter), BF),
            ],
            us=2,
            name="norm_second_back",
        )

    def pieces(s):
        cut = run(
            pieces_body,
            [place],
            [both_cores(products[s])],
            [((size, span), BF)] * 4,
            us=0.6,
            name="pieces",
        )
        mixture_grads[s] = redistribute(cut)

    def exchange_packs():
        for mine, theirs in packs:
            exchanged.extend([mine, swap(later(theirs), "tp", 4, CORE)])

    def feed_grad(key, kinds):
        count = len(kinds) * units
        reductions[key] = Reduction(
            *run(
                functools.partial(feed_grad_body, units, kinds),
                [place],
                [*exchanged, cotangent],
                [((count, half), F32), ((count, half), BF)],
                us=1.7 * len(kinds),
                name="feed_grad" + str(len(kinds)),
            )
        )

    def attend_back(s):
        _, o_full, lse = attended[s]
        d[s] = redistribute(
            run(
                functools.partial(attend_back_body, s, span),
                [place, lengths],
                [*keys, *rest[s], *mixture_grads[s], o_full, lse, cosine, sine],
                [((3 * size, span), BF)] * 4,
                scratch=[
                    pltpu.VMEM((4, span, size), BF),
                    pltpu.VMEM((4, size, span), BF),
                    pltpu.VMEM((4, span, size), BF),
                    pltpu.VMEM((4, size, span), F32),
                    pltpu.VMEM((4, span, size), F32),
                    pltpu.VMEM((4, span, size), F32),
                    pltpu.VMEM((4, span, size), BF),
                    pltpu.VMEM((4, span, size), BF),
                    pltpu.VMEM((4, span), F32),
                ],
                us=13,
                name="attend_back",
            )
        )

    def project_back(s):
        keep, send, stacks[s], gain_first[s] = run(
            project_back_body,
            [place],
            [*d[s], Part(inputs, s), *query_w, *key_w, *value_w],
            [
                ((quarter, width), F32),
                ((quarter, width), BF),
                ((3 * heads_width, span), BF),
                ((1, width), F32),
            ],
            us=2.4,
            name="project_back",
        )
        partials[s] = (keep, swap(send, "tp", 4, CORE))

    def project_sum(s):
        (mine,) = run(
            add_body, [], partials[s], [((quarter, width), BF)], us=0.4, name="project_sum"
        )
        back_sums[s] = (mine, swap(mine, "tp", 4, ROW))

    def first_back(s):
        (own,) = run(
            first_back_body,
            [place],
            [*back_sums[s], Part(inputs, s), middle_grads[s], first_gain],
            [((quarter, width), BF)],
            us=1.3,
            name="norm_first_back",
        )
        inputs_own[s] = (own, swap(own, "tp", 4, CORE))

    def exchange_branches():
        made["branches"] = [
            b for s in both for b in (branches[s], swap(later(branches[s]), "tp", 4, CORE))
        ]

    def attention_grad():
        sums = [gain_first[0], gain_first[1], gain_second[0], gain_second[1]]
        reductions["A"] = Reduction(
            *run(
                attention_grad_body,
                [place],
                [stacks[0], stacks[1], normed_first, *sums, *mixtures, *made["branches"]],
                [
                    ((rows + 16 + heads_width, half), F32),
                    ((rows + 16 + heads_width, half), BF),
                ],
                us=4.5,
                name="attention_grad",
            )
        )

    def output_start():
        made["out"] = swap(later(jnp.stack([f[1] for f in feeds])), "tp", 4, ROW)

    def output_own():
        (own,) = run(
            output_body,
            [place],
            [*[f[0] for f in feeds], *[f[1] for f in feeds], made["out"]],
            [((sequences, quarter, width), BF)],
            name="output",
        )
        made["out"] = (own, swap(own, "tp", 4, CORE))

    def output_join():
        (made["output"],) = run(
            join_stacked_body, [place], made["out"], [(inputs.shape, BF)], name="output_join"
        )

    def gradient_join():
        (made["gradient"],) = run(
            join_body,
            [place],
            [*inputs_own[0], *inputs_own[1]],
            [(inputs.shape, BF)],
            name="gradient_join",
        )

    steps = {
        "EX": exchange_packs,
        "FG1": lambda: feed_grad("I", (1,)),
        "FG2": lambda: feed_grad("O", (2, 0)),
        "BR": exchange_branches,
        "AT": attention_grad,
        "OT": output_start,
        "OO": output_own,
        "OJ": output_join,
        "JG": gradient_join,
    }
    for s in both:
        steps["SB" + str(s)] = functools.partial(second_back, s)
        steps["PC" + str(s)] = functools.partial(pieces, s)
        steps["AB" + str(s)] = functools.partial(attend_back, s)
        steps["PB" + str(s)] = functools.partial(project_back, s)
        steps["PS" + str(s)] = functools.partial(project_sum, s)
        steps["FB" + str(s)] = functools.partial(first_back, s)
    for line in ORDER:
        for step in line.split():
            if step in steps:
                steps[step]()
            else:
                stage = ("first", "second", "third", "fourth")[int(step[1]) - 1]
                getattr(reductions[step[0]], stage)()
    inner_grad, other_grad, attention_grad = (reductions[k] for k in "IOA")
    output, input_gradient = made["output"], made["gradient"]
    if pairs:
        lifting_gradient, down_gradient = run(
            functools.partial(feed_end_body, low),
            [place],
            [inner_grad.a, inner_grad.b, other_grad.a, other_grad.b],
            [((2, units, half), F32), ((units, half), F32)],
            us=2.5,
            name="feed_end",
        )
        triple_gradient, mixing_gradient, gain_parts = run(
            functools.partial(attention_end_body, low),
            [place],
            [attention_grad.a, attention_grad.b],
            [((3, half, heads_width), F32), ((heads_width, half), F32), ((2, half), F32)],
            us=2,
            name="attention_end",
        )
    else:
        lifting_gradient = jnp.stack([inner_grad.a, other_grad.a[:units]])
        down_gradient = other_grad.a[units:]
        total = attention_grad.a
        gain_parts = total[rows : rows + 2]
        triple_gradient = total[:rows].reshape(3, heads_width, -1).transpose(0, 2, 1)
        mixing_gradient = total[rows + 16 :]
    gain_parts = jnp.sum(lax.all_gather(gain_parts, "tp"), axis=0)
    lifting_gradient = lifting_gradient.transpose(2, 0, 1)
    triple_gradient = triple_gradient.transpose(1, 0, 2)

    return (
        output,
        input_gradient,
        gain_parts[0],
        triple_gradient,
        mixing_gradient,
        gain_parts[1],
        lifting_gradient,
        down_gradient,
    )


def solution(mesh):
    in_specs = (
        P("fsdp", "ctx", None),
        P("fsdp", "ctx", None),
        P("fsdp"),
        P("fsdp"),
        P("fsdp", None, "tp"),
        P("tp", "fsdp"),
        P("fsdp"),
        P("fsdp", None, "tp"),
        P("tp", "fsdp"),
    )
    out_specs = (
        P("fsdp", "ctx", None),
        P("fsdp", "ctx", None),
        P("fsdp"),
        P("fsdp", None, "tp"),
        P("tp", "fsdp"),
        P("fsdp"),
        P("fsdp", None, "tp"),
        P("tp", "fsdp"),
    )
    return jax.shard_map(
        functools.partial(on_device, sizes=dict(mesh.shape)),
        mesh=mesh,
        in_specs=in_specs,
        out_specs=out_specs,
        check_vma=False,
    )
```

```python
import functools

import jax
import jax.numpy as jnp
from jax import lax
from jax.experimental import pallas as pl
from jax.experimental.pallas import tpu as pltpu
from jax.sharding import PartitionSpec as P

H = 16
NORM_EPS = 1e-05
ROPE_BASE = 160000.0
MASKED = -1e30
LOG2E = 1.4426950408889634
BF = jnp.bfloat16
F32 = jnp.float32
FLOPS_PER_US = 1153e6
SCALE = 0.764
WEIGHTS = {"attend_back": 25.94, "attention_grad": 16.5, "feed": 1.008, "feed_grad1": 5.67, "gradient_join": 4.874, "halve": 6.466, "mix": 2.703, "norm_first_back": 0.2153, "norm_second_back": 0.9553, "output": 0.969, "output_join": 0.1857, "pieces": 0.09989, "project_back": 4.301, "project_sum": 0.246, "sum_ctx": 4.169}
WAIT_KEYS, WAIT_REST, WAIT_MIXING = (1,), (1,), True
FETCH = {"keys": "mixing", "first": "feed"}
ORDER = (
    "SB0 PC0 SB1 EX",
    "AB0 FG1 PC1 FG2",
    "I1 AB1 I2 BR",
    "PB0 O1 PS0 PB1",
    "FB0 OT AT I3",
    "PS1 O2 I4 FB1",
    "A1 O3 JG OO",
    "A2 O4 A3 A4",
    "OJ",
)
CORE, ROW = 1, 2


def nn(a, b):
    return lax.dot_general(a, b, (((1,), (0,)), ((), ())), preferred_element_type=F32)


def nt(a, b):
    return lax.dot_general(a, b, (((1,), (1,)), ((), ())), preferred_element_type=F32)


def tn(a, b):
    return lax.dot_general(a, b, (((0,), (0,)), ((), ())), preferred_element_type=F32)


def swap(array, axis, size, step):
    return lax.ppermute(array, axis, [(i, i ^ step) for i in range(size)])


def part(start, size):
    return pl.ds(pl.multiple_of(start * size, size), size)


def piece(refs, z, m):
    return refs[m] if len(refs) == 4 else refs[0].at[z ^ m]


class Part:
    def __init__(self, array, index):
        self.array, self.index = array, index


class Sequence:
    def __init__(self):
        self.last = None

    def __call__(self, body, scalars, arrays, outs, scratch=(), us=1, name=None, wait=(), mib=16):
        operands = [a.array if isinstance(a, Part) else a for a in arrays]
        specs = [pl.BlockSpec(memory_space=pltpu.VMEM)] * len(arrays)
        after = list(wait) + ([] if self.last is None else [self.last])
        first = len(scalars) + len(arrays)

        def run(*refs):
            taken = refs[len(scalars) : first]
            taken = [
                r.at[a.index] if isinstance(a, Part) else r
                for r, a in zip(taken, arrays, strict=True)
            ]
            body(*refs[: len(scalars)], *taken, *refs[first + len(after) :])

        results = pl.pallas_call(
            run,
            out_shape=[jax.ShapeDtypeStruct(s, t) for s, t in outs],
            in_specs=[pl.BlockSpec(memory_space=pltpu.SMEM)] * len(scalars)
            + specs
            + [pl.BlockSpec(memory_space=pl.ANY)] * len(after),
            out_specs=[pl.BlockSpec(memory_space=pltpu.VMEM)] * len(outs),
            scratch_shapes=list(scratch),
            compiler_params=pltpu.CompilerParams(vmem_limit_bytes=mib << 20),
            cost_estimate=pl.CostEstimate(
                flops=int(WEIGHTS.get(name, us) * SCALE * FLOPS_PER_US), bytes_accessed=0, transcendentals=0
            ),
            name=name,
        )(*scalars, *operands, *after)
        self.last = min(results, key=lambda r: r.size)
        return results


def whole_gain(gain, xi):
    own, other = gain[0:1, :].astype(F32), gain[1:2, :].astype(F32)
    low = jnp.where(xi == 0, own, other)
    high = jnp.where(xi == 0, other, own)
    return jnp.concatenate([low, high], axis=1)


def norm_body(place, x, gain, out):
    gain_row = whole_gain(gain, place[2])
    step = 256
    for s in range(x.shape[0]):

        def block(i, carry, s=s):
            at = part(i, step)
            v = x[s, at, :].astype(F32)
            center = v - jnp.mean(v, axis=-1, keepdims=True)
            spread = jnp.mean(center * center, axis=-1, keepdims=True)
            out[s, at, :] = (center * lax.rsqrt(spread + NORM_EPS) * gain_row).astype(BF)
            return carry

        lax.fori_loop(0, x.shape[1] // step, block, 0)


def project_body(size, kinds, place, *refs):
    normed, cosine, sine = refs[0:3]
    weights = refs[3 : 3 + 2 * len(kinds)]
    outs, heads = refs[3 + 2 * len(kinds) : -1], refs[-1]
    count = len(outs)
    half = weights[0].shape[0]
    z, xi = place[0], place[2]
    blocks = normed.shape[0] if len(normed.shape) == 3 else 1
    span = normed.shape[-2]
    for s in range(blocks):
        rows = slice(s * span, (s + 1) * span)
        source = normed.at[s] if len(normed.shape) == 3 else normed
        n_own = source[:, part(xi, half)]
        n_other = source[:, part(1 - xi, half)]
        for i, rotated in enumerate(kinds):
            acc = nt(weights[2 * i][...].T, n_own) + nt(weights[2 * i + 1][...].T, n_other)
            for h in range(count):
                u = acc[h * size : (h + 1) * size]
                if rotated:
                    u1, u2 = u[: size // 2], u[size // 2 :]
                    co, si = cosine[...], sine[...]
                    u = jnp.concatenate([u1 * co - u2 * si, u2 * co + u1 * si], axis=0)
                heads[h, i * size : (i + 1) * size, rows] = u.astype(BF)
    for m in range(count):
        outs[m][...] = heads[z ^ m]


def attend_body(s, span, place, lengths, *refs):
    k, qv = refs[0:4], refs[4:8]
    *o, o_full, lse, keys, values, top, total = refs[8:]
    z = place[0]
    size = k[0].shape[0]
    cols = slice(s * span, (s + 1) * span)
    values[:, size:, :] = jnp.ones((4, values.shape[1] - size, span), BF)
    for m in range(4):
        keys[z ^ m] = k[m][:, cols].T
        values[z ^ m, :size, :] = qv[m][size:, :]
    top[...] = jnp.full_like(top, MASKED)
    total[...] = jnp.zeros_like(total)
    length = lengths[s]
    full = length // span
    rest = length - full * span
    unit = size**-0.5 * LOG2E

    def step(j, limit):
        key, value = keys[j], values[j]
        for m in range(4):
            raw = nn(key, qv[m][:size, :])
            if limit is not None:
                raw = jnp.where(lax.broadcasted_iota(jnp.int32, raw.shape, 0) < limit, raw, MASKED)
            before = top[m : m + 1, :]
            peak = jnp.maximum(before, jnp.max(raw, axis=0, keepdims=True))
            p = jnp.exp2((raw - peak) * unit)
            top[m : m + 1, :] = peak
            total[m] = total[m] * jnp.exp2((before - peak) * unit) + nn(value, p.astype(BF))

    def whole(j, carry):
        step(j, None)
        return carry

    lax.fori_loop(0, full, whole, 0)

    @pl.when(rest > 0)
    def _():
        step(full, rest)

    for m in range(4):
        normaliser = total[m, size : size + 1, :]
        result = total[m, :size, :] / normaliser
        o_full[m] = result
        piece(o, z, m)[...] = result.astype(BF)
        lse[m : m + 1, :] = top[m : m + 1, :] * unit + jnp.log(normaliser) * LOG2E


def attend_back_body(s, span, place, lengths, *refs):
    k, qv = refs[0:4], refs[4:8]
    keys, keys_t, values, d_query, d_key, d_value, queries, grads, delta = refs[-9:]
    count = (len(refs) - 21) // 2
    do, out = refs[8 : 8 + count], refs[12 + count : -9]
    o_full, lse, cosine, sine = refs[8 + count : 12 + count]
    z = place[0]
    size = k[0].shape[0]
    cols = slice(s * span, (s + 1) * span)
    for m in range(4):
        keys[z ^ m] = k[m][:, cols].T
        keys_t[z ^ m] = k[m][:, cols]
        values[z ^ m] = qv[m][size:, :].T
        queries[m] = qv[m][:size, :].T
        grads[m] = piece(do, z, m)[...].T
        delta[m : m + 1, :] = jnp.sum(piece(do, z, m)[...].astype(F32) * o_full[m], axis=0, keepdims=True)
    d_query[...] = jnp.zeros_like(d_query)
    d_key[...] = jnp.zeros_like(d_key)
    d_value[...] = jnp.zeros_like(d_value)
    length = lengths[s]
    full = length // span
    rest = length - full * span
    factor = size**-0.5

    def step(j, limit):
        key, key_t, value = keys[j], keys_t[j], values[j]
        for m in range(4):
            raw = nn(key, qv[m][:size, :])
            if limit is not None:
                raw = jnp.where(lax.broadcasted_iota(jnp.int32, raw.shape, 0) < limit, raw, MASKED)
            p = jnp.exp2(raw * (factor * LOG2E) - lse[m : m + 1, :])
            dp = nn(value, piece(do, z, m)[...])
            ds = (p * (dp - delta[m : m + 1, :])).astype(BF)
            d_value[j] += nn(p.astype(BF), grads[m])
            d_key[j] += nn(ds, queries[m])
            d_query[m] += nn(key_t, ds)

    def whole(j, carry):
        step(j, None)
        return carry

    lax.fori_loop(0, full, whole, 0)

    @pl.when(rest > 0)
    def _():
        step(full, rest)

    def back(w, j):
        at = part(j, span)
        co, si = cosine[:, at], sine[:, at]
        w1, w2 = w[: size // 2] * factor, w[size // 2 :] * factor
        return jnp.concatenate([w1 * co + w2 * si, w2 * co - w1 * si], axis=0).astype(BF)

    for m in range(4):
        j = z ^ m
        target = piece(out, z, m)
        target[0:size, :] = back(d_query[m], j)
        target[size : 2 * size, :] = back(d_key[j].T, j)
        target[2 * size :, :] = d_value[j].T.astype(BF)


def heads_body(place, *refs):
    *o, mixed = refs
    size = mixed.shape[0] // 4
    for m in range(4):
        mixed[part(place[0] ^ m, size), :] = piece(o, place[0], m)[...]


def mix_body(place, mixed, *refs):
    *weights, out = refs
    c, xi = place[1], place[2]
    width, half = weights[0].shape
    rows = out.shape[0]
    left = [mixed[part(at, width), part(c, rows)].T for at in (c, 1 - c)]
    for side, hi in ((0, xi), (1, 1 - xi)):
        total = nn(left[0], weights[side][...]) + nn(left[1], weights[2 + side][...])
        out[:, part(hi, half)] = total.astype(BF)


def add_body(a, b, out):
    out[...] = (a[...].astype(F32) + b[...].astype(F32)).astype(out.dtype)


def feed_body(place, mine, theirs, x, gain, cot, *refs):
    weights = refs[0:4]
    middle, out, out_grad, *packs = refs[4:]
    c, xi = place[1], place[2]
    rows, width = middle.shape
    half = width // 2
    units = weights[0].shape[0] // 3
    lanes = (packs[0].shape[1] - width) // 3
    token_rows = part(c, rows)
    v = x[token_rows, :].astype(F32) + (mine[...].astype(F32) + theirs[...].astype(F32))
    middle[...] = v
    center = v - jnp.mean(v, axis=-1, keepdims=True)
    spread = jnp.mean(center * center, axis=-1, keepdims=True)
    n = (center * lax.rsqrt(spread + NORM_EPS) * whole_gain(gain, place[2])).astype(BF)
    columns = (part(xi, half), part(1 - xi, half))
    packs[0][:, :width] = n
    packs[1][:, :width] = n
    totals, totals_grad = [None, None], [None, None]
    for i, pack in enumerate(packs):
        sides = weights[2 * i : 2 * i + 2]

        def over(left, rows_of, sides=sides):
            return sum(nt(left(cols), w[rows_of, :]) for w, cols in zip(sides, columns))

        inner, gate, down = (slice(k * units, (k + 1) * units) for k in range(3))
        a = over(lambda cols, pack=pack: pack[:, cols], inner)
        b = over(lambda cols, pack=pack: pack[:, cols], gate)
        dh = over(lambda cols: cot[token_rows, cols], down)
        cdf = 0.5 * (1.0 + lax.erf(a * (0.5**0.5)))
        act = a * cdf
        slope = cdf + a * jnp.exp(-0.5 * a * a) * (0.5 * 2.0**0.5 / jnp.pi**0.5)
        h = (act * b).astype(BF)
        da = (dh * b * slope).astype(BF)
        db = (dh * act).astype(BF)
        for k, value in enumerate((h, da, db)):
            pack[:, width + k * lanes : width + k * lanes + units] = value
        for side, w in enumerate(sides):
            term = nn(da, w[inner, :]) + nn(db, w[gate, :])
            totals_grad[side] = term if i == 0 else totals_grad[side] + term
            term = nn(h, w[down, :])
            totals[side] = term if i == 0 else totals[side] + term
    for side, cols in enumerate(columns):
        out_grad[:, cols] = totals_grad[side].astype(BF)
        out[:, cols] = totals[side].astype(BF)


def feed_grad_body(units, kinds, place, *refs):
    *packs, cot, keep, send = refs
    c, xi = place[1], place[2]
    half = keep.shape[1]
    rows, lanes = packs[0].shape
    lanes = (lanes - 2 * half) // 3
    for target, hi in ((send, 1 - xi), (keep, xi)):
        for row, kind in enumerate(kinds):
            total = None
            for i, pack in enumerate(packs):
                start = 2 * half + kind * lanes
                if kind == 0:
                    right = cot[i // 2, part(c if i % 2 == 0 else 1 - c, rows), part(hi, half)]
                else:
                    right = pack[:, part(hi, half)]
                term = tn(pack[:, start : start + units], right)
                total = term if total is None else total + term
            target[row * units : (row + 1) * units, :] = total.astype(target.dtype)


def attention_grad_body(place, *refs):
    stacks, (normed,), gains, mixed, branches = refs[0:2], refs[2:3], refs[3:7], refs[7:9], refs[9:13]
    keep, send = refs[13:]
    c, xi = place[1], place[2]
    half = keep.shape[1]
    rows = stacks[0].shape[0]
    width = rows // 3
    under = keep.shape[0] - rows - width
    tokens = branches[0].shape[0]
    for target, hi in ((send, 1 - xi), (keep, xi)):
        cols = part(hi, half)
        total = nn(stacks[0][...], normed[0, :, cols]) + nn(stacks[1][...], normed[1, :, cols])
        target[0:rows, :] = total.astype(target.dtype)
        first = gains[0][:, cols] + gains[1][:, cols]
        second = 0.5 * (gains[2][:, cols] + gains[3][:, cols])
        which = lax.broadcasted_iota(jnp.int32, (under, half), 0)
        both = jnp.where(which == 0, first, jnp.where(which == 1, second, 0.0))
        target[rows : rows + under, :] = both.astype(target.dtype)
        total = None
        for s in range(2):
            for side, at in ((0, c), (1, 1 - c)):
                left = mixed[s][part(c, width), part(at, tokens)]
                term = nn(left, branches[2 * s + side][:, cols])
                total = term if total is None else total + term
        target[rows + under :, :] = total.astype(target.dtype)


def halve_body(which, place, a, b, keep, send):
    columns = keep.shape[1]
    for target, at in ((send, 1 - place[which]), (keep, place[which])):
        cols = part(at, columns)
        total = a[:, cols].astype(F32) + b[:, cols].astype(F32)
        target[...] = total.astype(target.dtype)


def unite_body(which, place, mine, theirs, out):
    columns = mine.shape[1]
    out[:, part(place[which], columns)] = mine[...].astype(out.dtype)
    out[:, part(1 - place[which], columns)] = theirs[...].astype(out.dtype)


def feed_end_body(which, place, mine0, theirs0, mine1, theirs1, lifting, down):
    columns = mine0.shape[1]
    units = down.shape[0]
    for first, second, at in ((mine0, mine1, place[which]), (theirs0, theirs1, 1 - place[which])):
        cols = part(at, columns)
        lifting[0, :, cols] = first[...].astype(F32)
        lifting[1, :, cols] = second[0:units, :].astype(F32)
        down[:, cols] = second[units:, :].astype(F32)


def attention_end_body(which, place, mine, theirs, triple, mixing, gains):
    columns = mine.shape[1]
    width = triple.shape[2]
    for part_of, at in ((mine, place[which]), (theirs, 1 - place[which])):
        cols = part(at, columns)
        for kind in range(3):
            value = part_of[kind * width : (kind + 1) * width, :]
            triple[kind, cols, :] = value.T.astype(F32)
        gains[:, cols] = part_of[3 * width : 3 * width + 16, :].astype(F32)[0:2]
        mixing[:, cols] = part_of[part_of.shape[0] - width :, :].astype(F32)


def norm_back(v, gain, grad):
    center = v - jnp.mean(v, axis=-1, keepdims=True)
    spread = jnp.mean(center * center, axis=-1, keepdims=True)
    r = lax.rsqrt(spread + NORM_EPS)
    xhat = center * r
    eg = grad * gain
    mean_eg = jnp.mean(eg, axis=-1, keepdims=True)
    mean_egx = jnp.mean(eg * xhat, axis=-1, keepdims=True)
    back = r * (eg - mean_eg - xhat * mean_egx)
    return back, jnp.sum(grad * xhat, axis=0, keepdims=True)


def second_back_body(place, mine, theirs, middle, cot, gain, *refs):
    *weights, middle_grad, branch, gain_grad, product = refs
    c, xi = place[1], place[2]
    rows = middle.shape[0]
    heads_width, half = weights[0].shape
    grad = mine[...].astype(F32) + theirs[...].astype(F32)
    back, total = norm_back(middle[...], whole_gain(gain, xi), grad)
    result = cot[part(c, rows), :].astype(F32) + back
    middle_grad[...] = result
    branch[...] = result.astype(BF)
    gain_grad[...] = total
    left, right = branch[:, part(xi, half)], branch[:, part(1 - xi, half)]
    for i, at in ((0, c), (1, 1 - c)):
        term = nt(weights[2 * i][...], left) + nt(weights[2 * i + 1][...], right)
        product[part(at, heads_width), :] = term.astype(BF)


def pieces_body(place, product, *outs):
    z, c = place[0], place[1]
    rows, columns = product.shape
    size = rows // 16
    for m in range(4):
        for k in range(2):
            rows_here = part(8 * k + 4 * c + (z ^ m), size)
            piece(outs, z, m)[:, k * columns : (k + 1) * columns] = product[rows_here, :]


def first_back_body(place, mine, theirs, x, middle_grad, gain, out):
    rows = middle_grad.shape[0]
    grad = mine[...].astype(F32) + theirs[...].astype(F32)
    back, _ = norm_back(x[part(place[1], rows), :].astype(F32), whole_gain(gain, place[2]), grad)
    out[...] = (middle_grad[...] + back).astype(BF)


def output_body(place, m0, m1, f0, f1, theirs, out):
    for s, (m, f) in enumerate(((m0, f0), (m1, f1))):
        out[s] = (m[...] + (f[...].astype(F32) + theirs[s].astype(F32))).astype(BF)


def join_body(place, *refs):
    *parts, out = refs
    rows = parts[0].shape[0]
    for s in range(len(parts) // 2):
        out[s, part(place[1], rows), :] = parts[2 * s][...]
        out[s, part(1 - place[1], rows), :] = parts[2 * s + 1][...]


def join_stacked_body(place, own, other, out):
    rows = own.shape[1]
    out[:, part(place[1], rows), :] = own[...]
    out[:, part(1 - place[1], rows), :] = other[...]


def project_back_body(place, *refs):
    *d, x = refs[:-10]
    weights, (keep, send, stacked, gain_grad) = refs[-10:-4], refs[-4:]
    c, rows = place[1], keep.shape[0]
    z, xi = place[0], place[2]
    half, width = weights[0].shape
    size = d[0].shape[-2] // 3
    for m in range(4):
        here = piece(d, z, m)
        for kind in range(3):
            at = part(kind * (width // size) + (z ^ m), size)
            stacked[at, :] = here[kind * size : (kind + 1) * size, :]
    for target, at in ((send, 1 - c), (keep, c)):
        tokens = stacked[:, part(at, rows)].T
        v = x[part(at, rows), :].astype(F32)
        mean = jnp.mean(v, axis=-1, keepdims=True)
        center = v - mean
        r = lax.rsqrt(jnp.mean(center * center, axis=-1, keepdims=True) + NORM_EPS)
        for side, hi in ((0, xi), (1, 1 - xi)):
            total = None
            for kind in range(3):
                term = nt(
                    tokens[:, kind * width : (kind + 1) * width], weights[2 * kind + side][...]
                )
                total = term if total is None else total + term
            cols = part(hi, half)
            target[:, cols] = total.astype(target.dtype)
            xhat = (x[part(at, rows), cols].astype(F32) - mean) * r
            sums = jnp.sum(total * xhat, axis=0, keepdims=True)
            if target is send:
                gain_grad[:, cols] = sums
            else:
                gain_grad[:, cols] += sums


def on_device(
    inputs,
    cotangent,
    lengths,
    attention_gain,
    triple_weight,
    mixing_weight,
    feedforward_gain,
    lifting_weight,
    down_weight,
    sizes,
):
    run = Sequence()
    pairs = sizes["fsdp"] == 2
    sequences, span, width = inputs.shape
    half = width // 2
    heads_width = triple_weight.shape[2]
    size = width // H
    heads = heads_width // size
    units = down_weight.shape[0]
    z = lax.axis_index("ctx")
    core = lax.axis_index("tp") % 2
    xi = lax.axis_index("fsdp") if pairs else jnp.int32(0)
    place = jnp.stack([z, core, xi, z % 2, z // 2]).astype(jnp.int32)
    quarter = span // 2
    both = range(sequences)

    def gather(array, axis):
        if pairs:
            return array, swap(array, "fsdp", 2, 1)
        full = lax.all_gather(array, "fsdp", axis=axis, tiled=True)
        return lax.split(full, [full.shape[axis] // 2] * 2, axis=axis)

    def over_fsdp(keep, send):
        if pairs:
            return keep, swap(send, "fsdp", 2, 1)
        full = jnp.concatenate([keep.astype(BF), send], axis=1)
        keep = lax.psum_scatter(full, "fsdp", scatter_dimension=1, tiled=True)
        return keep, jnp.zeros_like(keep)

    def added(a, b, kind, name):
        return run(add_body, [], [a, b], [(b.shape, kind)], name=name)[0]

    cores = [[0, 1], [2, 3]]

    def both_cores(array):
        return lax.all_gather(array, "tp", axis_index_groups=cores, axis=0, tiled=True)

    def redistribute(pieces):
        moved = {m: swap(pieces[m], "ctx", 4, m) for m in (2, 3, 1)}
        return [pieces[0], moved[1], moved[2], moved[3]]

    low, high = 3, 4

    class Reduction:
        def __init__(self, keep, send):
            self.a, self.b = over_fsdp(keep, send)
            if not pairs:
                self.a = lax.psum(self.a, "ctx").astype(F32)

        def halve(self, which, step):
            if not pairs:
                return
            rows, columns = self.a.shape
            shape = (rows, columns // 2)
            self.a, send = run(
                functools.partial(halve_body, which),
                [place],
                [self.a, self.b],
                [(shape, F32), (shape, BF)],
                us=1,
                name="halve",
            )
            self.b = swap(send, "ctx", 4, step)

        def unite(self, which, kind):
            if not pairs:
                return
            rows, columns = self.b.shape
            shape = (rows, columns * 2)
            (self.a,) = run(
                functools.partial(unite_body, which),
                [place],
                [self.a, self.b],
                [(shape, kind)],
                us=0.7,
                name="unite",
            )

        def first(self):
            self.halve(low, 1)

        def second(self):
            self.halve(high, 2)

        def third(self):
            if not pairs:
                return
            (self.a,) = run(
                add_body, [], [self.a, self.b], [(self.b.shape, BF)], us=0.4, name="sum_ctx"
            )
            self.b = swap(self.a, "ctx", 4, 2)

        def fourth(self):
            if not pairs:
                return
            self.unite(high, BF)
            self.b = swap(self.a, "ctx", 4, 1)

    key_w = gather(triple_weight[:, 1], 0)
    gains_own, gains_other = gather(jnp.stack([attention_gain, feedforward_gain]), 1)
    first_gain = jnp.stack([gains_own[0], gains_other[0]])
    second_gain = jnp.stack([gains_own[1], gains_other[1]])

    full_length = span * sizes["ctx"]
    frequency = ROPE_BASE ** (-2.0 * jnp.arange(size // 2, dtype=F32) / size)
    angles = frequency[:, None] * jnp.arange(full_length, dtype=jnp.int32).astype(F32)[None, :]
    cosine, sine = jnp.cos(angles), jnp.sin(angles)
    cosine_here = lax.dynamic_slice_in_dim(cosine, z * span, span, 1)
    sine_here = lax.dynamic_slice_in_dim(sine, z * span, span, 1)

    (normed_first,) = run(
        norm_body, [place], [inputs, first_gain], [(inputs.shape, BF)], name="norm_first"
    )

    def later(array):
        return lax.optimization_barrier((array, run.last))[0]

    query_w = gather(later(triple_weight[:, 0]), 0)
    value_w = gather(later(triple_weight[:, 2]), 0)

    def project(normed, kinds, weights, columns, wait=()):
        return redistribute(
            run(
                functools.partial(project_body, size, kinds),
                [place],
                [normed, cosine_here, sine_here, *weights],
                [((len(kinds) * size, columns), BF)] * heads,
                scratch=[pltpu.VMEM((heads, len(kinds) * size, columns), BF)],
                us=1.3,
                wait=wait,
                name="project",
            )
        )

    keys = project(normed_first, (True,), key_w, sequences * span)
    first, second = Part(normed_first, 0), Part(normed_first, 1)
    feed_own = jnp.concatenate(
        [lifting_weight[:, 0].T, lifting_weight[:, 1].T, down_weight], axis=0
    )
    fetched = {}

    def fetch(point):
        for name in FETCH.get(point, "").split():
            source = {"mixing": mixing_weight, "feed": feed_own}[name]
            fetched[name] = gather(later(source), 1)

    fetch("keys")
    rest = [project(first, (True, False), (*query_w, *value_w), span, [keys[i] for i in WAIT_KEYS])]
    fetch("first")
    waits = [keys[i] for i in (1, 2, 3) if i not in WAIT_KEYS]
    waits += [rest[0][i] for i in WAIT_REST]
    waits += [fetched["mixing"][1]] if WAIT_MIXING and "mixing" in fetched else []
    rest.append(project(second, (True, False), (*query_w, *value_w), span, waits))
    fetch("second")

    attended = []

    def attend(s, wait):
        *o, o_full, lse = run(
            functools.partial(attend_body, s, span),
            [place, lengths],
            [*keys, *rest[s]],
            [*[((size, span), BF)] * 4, ((4, size, span), F32), ((4, span), F32)],
            scratch=[
                pltpu.VMEM((4, span, size), BF),
                pltpu.VMEM((4, size + 16, span), BF),
                pltpu.VMEM((4, span), F32),
                pltpu.VMEM((4, size + 16, span), F32),
            ],
            us=10,
            wait=wait,
            name="attend",
        )
        attended.append((redistribute(o), o_full, lse))

    attend(0, [])
    fetch("attend")
    mixing_w, feed_w = fetched["mixing"], fetched["feed"]
    attend(1, [])

    mixtures, sums, mixing_all = [], [], list(mixing_w)

    def mix(s, wait):
        (mixed,) = run(
            heads_body,
            [place],
            attended[s][0],
            [((heads_width, span), BF)],
            us=0.6,
            wait=wait,
            name="heads",
        )
        if s == 0:
            mixing_all.extend(swap(later(w), "tp", 4, CORE) for w in mixing_w)
        mixed = both_cores(mixed)
        mixtures.append(mixed)
        (mine,) = run(
            mix_body, [place], [mixed, *mixing_all], [((quarter, width), BF)], us=1, name="mix"
        )
        sums.append((mine, swap(mine, "tp", 4, ROW)))

    mix(0, [])
    feed_theirs = [swap(later(w), "tp", 4, CORE) for w in feed_w]
    mix(1, [])

    feeds, grads, packs = [], [], []
    lanes = -(-units // 128) * 128
    for s in both:
        feed = run(
            feed_body,
            [place],
            [*sums[s], Part(inputs, s), second_gain, Part(cotangent, s), *feed_w, *feed_theirs],
            [
                ((quarter, width), F32),
                ((quarter, width), BF),
                ((quarter, width), BF),
                ((quarter, width + 3 * lanes), BF),
                ((quarter, width + 3 * lanes), BF),
            ],
            us=6.6,
            name="feed",
        )
        feeds.append(feed)
        grads.append((feed[2], swap(feed[2], "tp", 4, ROW)))
        packs.append((feed[3], feed[4]))
    rows = 3 * heads_width
    branches, middle_grads, gain_second, mixture_grads = {}, {}, {}, {}
    products, exchanged, reductions, d, partials = {}, [], {}, {}, {}
    stacks, gain_first, back_sums, inputs_own, made = {}, {}, {}, {}, {}

    def second_back(s):
        middle_grads[s], branches[s], gain_second[s], products[s] = run(
            second_back_body,
            [place],
            [*grads[s], feeds[s][0], Part(cotangent, s), second_gain, *mixing_all],
            [
                ((quarter, width), F32),
                ((quarter, width), BF),
                ((1, width), F32),
                ((2 * heads_width, quarter), BF),
            ],
            us=2,
            name="norm_second_back",
        )

    def pieces(s):
        cut = run(
            pieces_body,
            [place],
            [both_cores(products[s])],
            [((size, span), BF)] * 4,
            us=0.6,
            name="pieces",
        )
        mixture_grads[s] = redistribute(cut)

    def exchange_packs():
        for mine, theirs in packs:
            exchanged.extend([mine, swap(later(theirs), "tp", 4, CORE)])

    def feed_grad(key, kinds):
        count = len(kinds) * units
        reductions[key] = Reduction(
            *run(
                functools.partial(feed_grad_body, units, kinds),
                [place],
                [*exchanged, cotangent],
                [((count, half), F32), ((count, half), BF)],
                us=1.7 * len(kinds),
                name="feed_grad" + str(len(kinds)),
            )
        )

    def attend_back(s):
        _, o_full, lse = attended[s]
        d[s] = redistribute(
            run(
                functools.partial(attend_back_body, s, span),
                [place, lengths],
                [*keys, *rest[s], *mixture_grads[s], o_full, lse, cosine, sine],
                [((3 * size, span), BF)] * 4,
                scratch=[
                    pltpu.VMEM((4, span, size), BF),
                    pltpu.VMEM((4, size, span), BF),
                    pltpu.VMEM((4, span, size), BF),
                    pltpu.VMEM((4, size, span), F32),
                    pltpu.VMEM((4, span, size), F32),
                    pltpu.VMEM((4, span, size), F32),
                    pltpu.VMEM((4, span, size), BF),
                    pltpu.VMEM((4, span, size), BF),
                    pltpu.VMEM((4, span), F32),
                ],
                us=13,
                name="attend_back",
            )
        )

    def project_back(s):
        keep, send, stacks[s], gain_first[s] = run(
            project_back_body,
            [place],
            [*d[s], Part(inputs, s), *query_w, *key_w, *value_w],
            [
                ((quarter, width), F32),
                ((quarter, width), BF),
                ((3 * heads_width, span), BF),
                ((1, width), F32),
            ],
            us=2.4,
            name="project_back",
        )
        partials[s] = (keep, swap(send, "tp", 4, CORE))

    def project_sum(s):
        (mine,) = run(
            add_body, [], partials[s], [((quarter, width), BF)], us=0.4, name="project_sum"
        )
        back_sums[s] = (mine, swap(mine, "tp", 4, ROW))

    def first_back(s):
        (own,) = run(
            first_back_body,
            [place],
            [*back_sums[s], Part(inputs, s), middle_grads[s], first_gain],
            [((quarter, width), BF)],
            us=1.3,
            name="norm_first_back",
        )
        inputs_own[s] = (own, swap(own, "tp", 4, CORE))

    def exchange_branches():
        made["branches"] = [
            b for s in both for b in (branches[s], swap(later(branches[s]), "tp", 4, CORE))
        ]

    def attention_grad():
        sums = [gain_first[0], gain_first[1], gain_second[0], gain_second[1]]
        reductions["A"] = Reduction(
            *run(
                attention_grad_body,
                [place],
                [stacks[0], stacks[1], normed_first, *sums, *mixtures, *made["branches"]],
                [
                    ((rows + 16 + heads_width, half), F32),
                    ((rows + 16 + heads_width, half), BF),
                ],
                us=4.5,
                name="attention_grad",
            )
        )

    def output_start():
        made["out"] = swap(later(jnp.stack([f[1] for f in feeds])), "tp", 4, ROW)

    def output_own():
        (own,) = run(
            output_body,
            [place],
            [*[f[0] for f in feeds], *[f[1] for f in feeds], made["out"]],
            [((sequences, quarter, width), BF)],
            name="output",
        )
        made["out"] = (own, swap(own, "tp", 4, CORE))

    def output_join():
        (made["output"],) = run(
            join_stacked_body, [place], made["out"], [(inputs.shape, BF)], name="output_join"
        )

    def gradient_join():
        (made["gradient"],) = run(
            join_body,
            [place],
            [*inputs_own[0], *inputs_own[1]],
            [(inputs.shape, BF)],
            name="gradient_join",
        )

    steps = {
        "EX": exchange_packs,
        "FG1": lambda: feed_grad("I", (1,)),
        "FG2": lambda: feed_grad("O", (2, 0)),
        "BR": exchange_branches,
        "AT": attention_grad,
        "OT": output_start,
        "OO": output_own,
        "OJ": output_join,
        "JG": gradient_join,
    }
    for s in both:
        steps["SB" + str(s)] = functools.partial(second_back, s)
        steps["PC" + str(s)] = functools.partial(pieces, s)
        steps["AB" + str(s)] = functools.partial(attend_back, s)
        steps["PB" + str(s)] = functools.partial(project_back, s)
        steps["PS" + str(s)] = functools.partial(project_sum, s)
        steps["FB" + str(s)] = functools.partial(first_back, s)
    for line in ORDER:
        for step in line.split():
            if step in steps:
                steps[step]()
            else:
                stage = ("first", "second", "third", "fourth")[int(step[1]) - 1]
                getattr(reductions[step[0]], stage)()
    inner_grad, other_grad, attention_grad = (reductions[k] for k in "IOA")
    output, input_gradient = made["output"], made["gradient"]
    if pairs:
        lifting_gradient, down_gradient = run(
            functools.partial(feed_end_body, low),
            [place],
            [inner_grad.a, inner_grad.b, other_grad.a, other_grad.b],
            [((2, units, half), F32), ((units, half), F32)],
            us=2.5,
            name="feed_end",
        )
        triple_gradient, mixing_gradient, gain_parts = run(
            functools.partial(attention_end_body, low),
            [place],
            [attention_grad.a, attention_grad.b],
            [((3, half, heads_width), F32), ((heads_width, half), F32), ((2, half), F32)],
            us=2,
            name="attention_end",
        )
    else:
        lifting_gradient = jnp.stack([inner_grad.a, other_grad.a[:units]])
        down_gradient = other_grad.a[units:]
        total = attention_grad.a
        gain_parts = total[rows : rows + 2]
        triple_gradient = total[:rows].reshape(3, heads_width, -1).transpose(0, 2, 1)
        mixing_gradient = total[rows + 16 :]
    gain_parts = jnp.sum(lax.all_gather(gain_parts, "tp"), axis=0)
    lifting_gradient = lifting_gradient.transpose(2, 0, 1)
    triple_gradient = triple_gradient.transpose(1, 0, 2)

    return (
        output,
        input_gradient,
        gain_parts[0],
        triple_gradient,
        mixing_gradient,
        gain_parts[1],
        lifting_gradient,
        down_gradient,
    )


def solution(mesh):
    in_specs = (
        P("fsdp", "ctx", None),
        P("fsdp", "ctx", None),
        P("fsdp"),
        P("fsdp"),
        P("fsdp", None, "tp"),
        P("tp", "fsdp"),
        P("fsdp"),
        P("fsdp", None, "tp"),
        P("tp", "fsdp"),
    )
    out_specs = (
        P("fsdp", "ctx", None),
        P("fsdp", "ctx", None),
        P("fsdp"),
        P("fsdp", None, "tp"),
        P("tp", "fsdp"),
        P("fsdp"),
        P("fsdp", None, "tp"),
        P("tp", "fsdp"),
    )
    return jax.shard_map(
        functools.partial(on_device, sizes=dict(mesh.shape)),
        mesh=mesh,
        in_specs=in_specs,
        out_specs=out_specs,
        check_vma=False,
    )
```
